32 devices in a mesh: gx: 16 (over z, x, core), gy: 2 (over y).
Axes of the slice: x: 2, y: 2, z: 4, core: 2. Of those that a mesh axis runs over, the one named last changes fastest.
Arguments:
- initial: float32 [64, 256, 512], P('gx', 'gy'), may hold values from -4 to 4
- kappa: float32 [64, 256, 512], P('gx', 'gy'), may hold values from 0.04 to 0.12
- velocity: float32 [64, 256, 512], P('gx', 'gy'), may hold values from 0.05 to 0.2
- rate: float32 [64, 256, 512], P('gx', 'gy'), may hold values from 0.05 to 0.3
Outputs:
- final: float32 [64, 256, 512], P('gx', 'gy')
The draws below stay inside these ranges and needn't reach their ends.
All inputs are finite; a program needn't handle non-finite values.
Results may differ from the reference program's by a relative error of at most 0.00002.
Values sent between devices are 32-bit elements; how exact they have to be, the bound alone decides.
No kernel may reach another device: no remote copies, remote signals or barrier semaphores. Data moves between devices by JAX's collectives and lax.ppermute only.
A program may use at most 64 MiB of HBM per device.

```python
import math
import jax
import jax.numpy as jnp

CX = 4
CZ = 512
STEPS = 4
ITERS = 2
NX = 64
NY = 256
N_GX = 16


def level_of(key, extent, split, smallest, top_value):
    def one(axis_at, parts):
        heights = jax.random.uniform(jax.random.fold_in(jax.random.fold_in(key, 6), axis_at), (parts,), jnp.float32, smallest / len(split), top_value / len(split))
        return jnp.repeat(jnp.exp(heights), extent[axis_at] // parts).reshape((-1,) + (1,) * (len(extent) - axis_at - 1))

    level = one(*split[0])
    for cut in split[1:]:
        level = level * one(*cut)
    return level


def gaussian(rng, extent, spread, most, cuts=(), held_as=jnp.bfloat16):
    drawn = jax.random.normal(rng, extent, jnp.float32) * spread
    if len(cuts) > 0:
        drawn = level_of(rng, extent, cuts, -0.22, 0.18) * drawn
    return jnp.clip(drawn, min=-most, max=most).astype(held_as)


def setup_inputs(seed: int = 0) -> dict:
    key_of = jax.random.split(jax.random.key(seed), 5)
    return {
        "initial": gaussian(key_of[0], (NX, NY, CZ), 1.0, 4.0, ((0, 16), (1, 2)), jnp.float32),
        "kappa": jnp.clip(0.04 + 0.08 * jax.random.uniform(key_of[1], (NX, NY, CZ), jnp.float32) ** level_of(key_of[1], (NX, NY, CZ), ((0, 16), (1, 2)), -0.2, 0.2), 0.04, 0.12),
        "velocity": jnp.clip(0.05 + 0.15 * jax.random.uniform(key_of[2], (NX, NY, CZ), jnp.float32) ** level_of(key_of[2], (NX, NY, CZ), ((0, 16), (1, 2)), -0.2, 0.2), 0.05, 0.2),
        "rate": jnp.clip(jnp.exp(math.log(0.3) - 1.7917595 * jax.random.uniform(key_of[3], (NX, NY, CZ), jnp.float32) ** level_of(key_of[3], (NX, NY, CZ), ((0, 16), (1, 2)), -0.2, 0.2)), 0.05, 0.3),
    }


robin_p = 0.6


def advance(field, kappa, velocity, rate, data_left, data_right):
    first = field[:, 0]
    last = field[:, -1]
    ghost_left = (data_left + first * (1.0 - robin_p / 2)) / (1.0 + robin_p / 2)
    ghost_right = (data_right + last * (1.0 - robin_p / 2)) / (1.0 + robin_p / 2)
    extended = jnp.concatenate([ghost_left[:, None], field, ghost_right[:, None]], axis=1)
    extended = jnp.pad(extended, ((0, 0), (0, 0), (1, 1), (1, 1)))
    center = extended[:, 1:-1, 1:-1, 1:-1]
    minus_x = extended[:, :-2, 1:-1, 1:-1]
    lap = extended[:, 2:, 1:-1, 1:-1] + minus_x
    lap = lap + extended[:, 1:-1, 2:, 1:-1] + extended[:, 1:-1, :-2, 1:-1]
    lap = lap + extended[:, 1:-1, 1:-1, 2:] + extended[:, 1:-1, 1:-1, :-2]
    lap = lap - 6.0 * center
    react = rate * center ** 3 / (1.0 + center * center)
    updated = center + kappa * lap - velocity * (center - minus_x) - react
    return updated, first, ghost_left, last, ghost_right


def reference(initial, kappa, velocity, rate):
    shape = (N_GX, CX, NY, CZ)
    start = initial.reshape(shape)
    kappa_s = kappa.reshape(shape)
    velocity_s = velocity.reshape(shape)
    rate_s = rate.reshape(shape)
    zero_plane = jnp.zeros((N_GX, NY, CZ), jnp.float32)
    data_left = [zero_plane] * STEPS
    data_right = [zero_plane] * STEPS
    field = start
    for sweep in range(ITERS):
        field = start
        traces = []
        for step in range(STEPS):
            field, first, ghost_left, last, ghost_right = advance(field, kappa_s, velocity_s, rate_s, data_left[step], data_right[step])
            traces.append((first, ghost_left, last, ghost_right))
        if sweep + 1 < ITERS:
            new_left = []
            new_right = []
            for step in range(STEPS):
                first, ghost_left, last, ghost_right = traces[step]
                toward_prev = (first - ghost_left) + robin_p * (first + ghost_left) / 2
                toward_next = (last - ghost_right) + robin_p * (last + ghost_right) / 2
                new_right.append(jnp.roll(toward_prev, -1, axis=0))
                new_left.append(jnp.roll(toward_next, 1, axis=0))
            data_left = new_left
            data_right = new_right
    return field.reshape(NX, NY, CZ)
```

```python
import functools

import jax
import jax.numpy as jnp
from jax import lax
from jax.experimental import pallas as pl
from jax.experimental.pallas import tpu as pltpu
from jax.sharding import PartitionSpec as P

robin_p = 0.6
own = (1.0 - robin_p / 2) / (1.0 + robin_p / 2)
far = ((1.0 - own) + robin_p * (1.0 + own) / 2) / (1.0 + robin_p / 2)

VMEM = pl.BlockSpec(memory_space=pltpu.VMEM)
ANY = pl.BlockSpec(memory_space=pl.ANY)
HALO = 4
ROWS = 8
LANES = 128


def parity(axis):
    return lax.rem(lax.axis_index(axis), 2)


def plane_at(d, odd):
    return d + odd * (3 - 2 * d)


def pick(odd, yes, no):
    return jnp.where(jnp.broadcast_to(odd == 1, yes.shape), yes, no)


def load(ref, index, tile):
    rows = pl.ds(tile * ROWS if isinstance(tile, int) else pl.multiple_of(tile * ROWS, ROWS), ROWS)
    return [ref[*index, rows, k : k + LANES] for k in range(0, ref.shape[-1], LANES)]


def store(ref, index, tile, pieces):
    rows = pl.ds(tile * ROWS if isinstance(tile, int) else pl.multiple_of(tile * ROWS, ROWS), ROWS)
    for k, piece in enumerate(pieces):
        ref[*index, rows, k * LANES : (k + 1) * LANES] = piece


def ghost(mine, received=None):
    if received is None:
        return [m * own for m in mine]
    return [r * far + m * own for r, m in zip(received, mine)]


def updated(odd, cur, before, after, toward, away, kappa, velocity, rate):
    row = lax.broadcasted_iota(jnp.int32, (ROWS, LANES), 0)
    lane = lax.broadcasted_iota(jnp.int32, (ROWS, LANES), 1)
    zero = jnp.zeros((ROWS, LANES), jnp.float32)
    out = []
    for k, c in enumerate(cur):
        up = pltpu.roll(jnp.where(row == ROWS - 1, before[k], c), 1, 0)
        down = pltpu.roll(jnp.where(row == 0, after[k], c), ROWS - 1, 0)
        low = cur[k - 1] if k else zero
        high = cur[k + 1] if k + 1 < len(cur) else zero
        left = pltpu.roll(jnp.where(lane == LANES - 1, low, c), 1, 1)
        right = pltpu.roll(jnp.where(lane == 0, high, c), LANES - 1, 1)
        minus_x = pick(odd, away[k], toward[k]) if toward is not None else away[k]
        lap = away[k] + toward[k]
        lap = lap + up + down
        lap = lap + left + right
        lap = lap - 6.0 * c
        square = c * c
        bottom = 1.0 + square
        inverse = pl.reciprocal(bottom, approx=True)
        inverse = inverse * (2.0 - bottom * inverse)
        react = rate[k] * c * (square * inverse)
        out.append(c + kappa[k] * lap - velocity[k] * (c - minus_x) - react)
    return out


def sweep(odd, wanted, source, coefs, margins, near, distant, sink, edge=True):
    needed = sorted({e for d in wanted for e in (d - 1, d, d + 1) if 0 <= e <= 3})
    tiles = source(wanted[0])[0].shape[-2] // ROWS
    last = tiles - 1

    def body(tile, edge_tile):
        if edge_tile:
            before, after = last - 1, 0
        else:
            before, after = lax.select(tile == 0, last, tile - 1), tile + 1
        state = {d: load(*source(d), tile) for d in needed}
        for d in wanted:
            cur = state[d]
            toward = state[d - 1] if d > 0 else ghost(cur, near(tile))
            away = state[d + 1] if d < 3 else ghost(cur, distant(tile))
            p = plane_at(d, odd)
            kvr = [load(ref, (*lead, p), 0 if edge_tile else tile) for ref, lead in (margins if edge_tile else coefs)]
            sink(d, tile, updated(odd, cur, load(*source(d), before), load(*source(d), after), toward, away, *kvr))

    def loop(tile, carry):
        body(tile, False)
        return carry

    lax.fori_loop(0, last, loop, 0)
    if edge:
        body(last, True)


def none(tile):
    return None


def pack_kernel(n_halo, initial, kappa, velocity, rate, plane, *rest):
    halos, (tiles, sems) = rest[:n_halo], rest[n_halo:]
    odd_x, odd_y = parity("gx"), parity("gy")
    rows = initial.shape[1]
    copies = [pltpu.make_async_copy(initial.at[plane_at(0, odd_x)], plane, sems.at[0])]
    for f, field in enumerate((initial, kappa, velocity, rate)):
        copies.append(pltpu.make_async_copy(field.at[:, :ROWS, :], tiles.at[f, 0], sems.at[1 + 2 * f]))
        copies.append(pltpu.make_async_copy(field.at[:, rows - ROWS :, :], tiles.at[f, 1], sems.at[2 + 2 * f]))
    for copy in copies:
        copy.start()
    for copy in copies[1:]:
        copy.wait()
    for f in range(4):
        first, last = tiles[f, 0, :, :HALO], tiles[f, 1, :, ROWS - HALO :]
        halos[0][4 * f : 4 * f + 4] = pick(odd_y, first, last)
        if n_halo > 1:
            halos[1][4 * f : 4 * f + 4] = pick(odd_y, last, first)
    copies[0].wait()


def first_kernel(n_halo, initial, kappa, velocity, rate, *rest):
    halos, (u0, u1, margin, message) = rest[:n_halo], rest[n_halo:]
    odd, odd_y = parity("gx"), parity("gy")
    rows = initial.shape[1]
    for f in range(4):
        one = halos[0][4 * f : 4 * f + 4]
        two = halos[1][4 * f : 4 * f + 4] if n_halo > 1 else jnp.zeros_like(one)
        edge = jnp.concatenate([pick(odd_y, two, one), pick(odd_y, one, two)], axis=1)
        if f == 0:
            u0[:, rows:, :] = edge
        else:
            margin[f - 1] = edge

    def copy(tile, carry):
        for p in range(4):
            store(u0, (p,), tile, load(initial, (p,), tile))
        return carry

    lax.fori_loop(0, rows // ROWS, copy, 0)

    def sink(d, tile, pieces):
        store(u1, (plane_at(d, odd),), tile, pieces)

    coefs = [(ref, ()) for ref in (kappa, velocity, rate)]
    margins = [(margin, (i,)) for i in range(3)]
    sweep(odd, [0, 1, 2, 3], lambda d: (u0, (plane_at(d, odd),)), coefs, margins, none, none, sink)
    p = plane_at(0, odd)
    message[:rows] = u1[p, :rows]
    zero = u0[p, rows:]
    one = u1[p, rows:]
    if n_halo > 1:
        message[rows : rows + ROWS] = zero
        message[rows + ROWS :] = one
    else:
        half = lax.broadcasted_iota(jnp.int32, zero.shape, 0) // HALO
        message[rows:] = jnp.where(half == odd_y, zero, pltpu.roll(one, HALO, 0))


def second_kernel(u0, u1, margin, kappa, velocity, rate, message2, message3, beside, u2):
    odd = parity("gx")
    rows = kappa.shape[1]
    coefs = [(ref, ()) for ref in (kappa, velocity, rate)]
    margins = [(margin, (i,)) for i in range(3)]

    def sink2(d, tile, pieces):
        store(u2, (plane_at(d, odd),), tile, pieces)
        if d == 0:
            store(message2, (), tile, pieces)
        if d == 3:
            store(beside, (2,), tile, pieces)

    sweep(odd, [0, 1, 2, 3], lambda d: (u1, (plane_at(d, odd),)), coefs, margins, none, none, sink2)

    def sink3(d, tile, pieces):
        if d == 0:
            store(message3, (), tile, pieces)
        if d == 3:
            store(beside, (3,), tile, pieces)

    sweep(odd, [0, 3], lambda d: (u2, (plane_at(d, odd),)), coefs, margins, none, none, sink3, edge=False)
    beside[3, rows:] = jnp.zeros(beside[3, rows:].shape, jnp.float32)
    beside[0] = u0[plane_at(3, odd)]
    beside[1] = u1[plane_at(3, odd)]


def third_kernel(n_halo, u0, u1, margin, kappa, velocity, rate, near0, near1, beside,
                 out, state, v1, v2, v3, edges, done, sems):
    odd, odd_y = parity("gx"), parity("gy")
    rows = kappa.shape[1]
    coefs = [(ref, ()) for ref in (kappa, velocity, rate)]
    margins = [(margin, (i,)) for i in range(3)]
    if n_halo > 1:
        edges[0] = near1[rows : rows + ROWS]
        edges[1] = near1[rows + ROWS :]
    else:
        edges[0] = near1[rows:]
        edges[1] = pltpu.roll(near1[rows:], HALO, 0)

    def near(step, ref):
        last = rows // ROWS
        return lambda tile: load(edges, (step,), 0) if isinstance(tile, int) and tile == last else load(ref, (), tile)

    def distant(step):
        return lambda tile: load(beside, (step,), tile)

    def sink1(d, tile, pieces):
        store(v1, (d // 3,), tile, pieces)

    def source1(d):
        return (v1, (d // 3,)) if d in (0, 3) else (u1, (plane_at(d, odd),))

    def sink2(d, tile, pieces):
        if d < 2:
            store(state, (d,), tile, pieces)
        else:
            store(v2, (d - 2,), tile, pieces)

    def source2(d):
        return (state, (d,)) if d < 2 else (v2, (d - 2,))

    def sink3(d, tile, pieces):
        if d < 3:
            store(state, (d + 1,), tile, pieces)
        else:
            store(v3, (), tile, pieces)

    def source3(d):
        return (state, (d + 1,)) if d < 3 else (v3, ())

    def sink4(d, tile, pieces):
        store(done, (d - 2,), tile, pieces)

    sweep(odd, [0, 3], lambda d: (u0, (plane_at(d, odd),)), coefs, margins, near(0, near0), distant(0), sink1)
    sweep(odd, [0, 1, 2, 3], source1, coefs, margins, near(1, near1), distant(1), sink2)
    sweep(odd, [1, 2, 3], source2, coefs, margins, none, distant(2), sink3)
    sweep(odd, [2, 3], source3, coefs, margins, none, distant(3), sink4, edge=False)
    copies = [pltpu.make_async_copy(done.at[d - 2], out.at[plane_at(d, odd)], sems.at[d - 2]) for d in (2, 3)]
    for copy in copies:
        copy.start()
    for copy in copies:
        copy.wait()


def fourth_kernel(state, margin, kappa, velocity, rate, near2, out_in, out, base, gain, v3, done, sem):
    del out_in
    odd = parity("gx")
    rows = kappa.shape[1]
    coefs = [(ref, ()) for ref in (kappa, velocity, rate)]
    margins = [(margin, (i,)) for i in range(3)]

    def sink3(d, tile, pieces):
        store(v3, (), tile, pieces)

    sweep(odd, [0], lambda d: (state, (d,)), coefs, margins, lambda tile: load(near2, (), tile), none, sink3)

    def source3(d):
        return (v3, ()) if d == 0 else (state, (d + 1,))

    def sink4(d, tile, pieces):
        store(done if d else base, (), tile, pieces)

    sweep(odd, [0, 1], source3, coefs, margins, none, none, sink4, edge=False)
    copy = pltpu.make_async_copy(done, out.at[plane_at(1, odd)], sem)
    copy.start()
    p = plane_at(0, odd)

    def gains(tile, carry):
        both = zip(load(kappa, (p,), tile), load(velocity, (p,), tile))
        store(gain, (), tile, [far * (k + pick(odd, jnp.zeros_like(v), v)) for k, v in both])
        return carry

    lax.fori_loop(0, rows // ROWS, gains, 0)
    copy.wait()


def last_kernel(base, gain, near3, out_in, out, done, sem):
    del out_in
    odd = parity("gx")
    done[...] = base[...] + gain[...] * near3[...]
    copy = pltpu.make_async_copy(done, out.at[plane_at(0, odd)], sem)
    copy.start()
    copy.wait()


def pairs(count, first, wrap):
    out = []
    for i in range(first, count, 2):
        if i + 1 < count or wrap:
            out += [(i, (i + 1) % count), ((i + 1) % count, i)]
    return out


def f32(*shape):
    return jax.ShapeDtypeStruct(shape, jnp.float32)


def call(kernel, out_shape, in_specs, out_specs, scratch=(), aliases=None, cells=0):
    return pl.pallas_call(
        kernel,
        out_shape=out_shape,
        in_specs=in_specs,
        out_specs=out_specs,
        scratch_shapes=scratch,
        input_output_aliases=aliases or {},
        cost_estimate=pl.CostEstimate(flops=25 * cells, bytes_accessed=16 * cells, transcendentals=cells),
        compiler_params=pltpu.CompilerParams(vmem_limit_bytes=24 * 1024 * 1024),
    )


def local(initial, kappa, velocity, rate):
    planes, rows, lanes = initial.shape
    full = rows + ROWS
    count_y = lax.axis_size("gy")
    count_x = lax.axis_size("gx")
    n_halo = 1 if count_y == 2 else 2
    plane = rows * lanes
    chips = pairs(count_x, 1, True)
    cores = pairs(count_x, 0, False)
    rows_pairs = [pairs(count_y, 0, False), pairs(count_y, 1, False)][:n_halo]

    plane0, *halos = call(
        functools.partial(pack_kernel, n_halo),
        [f32(rows, lanes)] + [f32(16, HALO, lanes)] * n_halo,
        [ANY] * 4,
        [ANY] + [VMEM] * n_halo,
        [pltpu.VMEM((4, 2, planes, ROWS, lanes), jnp.float32), pltpu.SemaphoreType.DMA((9,))],
        cells=plane // 2,
    )(initial, kappa, velocity, rate)
    near0 = lax.ppermute(plane0, "gx", chips)
    halos = [lax.ppermute(halo, "gy", which) for halo, which in zip(halos, rows_pairs)]
    u0, u1, margin, message1 = call(
        functools.partial(first_kernel, n_halo),
        [f32(planes, full, lanes), f32(planes, full, lanes), f32(3, planes, ROWS, lanes), f32(rows + ROWS * n_halo, lanes)],
        [VMEM] * (4 + n_halo),
        [VMEM] * 4,
        cells=4 * plane,
    )(initial, kappa, velocity, rate, *halos)
    near1 = lax.ppermute(message1, "gx", chips)
    message2, message3, beside = call(
        second_kernel,
        [f32(full, lanes), f32(rows, lanes), f32(4, full, lanes)],
        [VMEM] * 6,
        [VMEM] * 3,
        [pltpu.VMEM((planes, full, lanes), jnp.float32)],
        cells=6 * plane,
    )(u0, u1, margin, kappa, velocity, rate)
    beside = lax.ppermute(beside, "gx", cores)
    message2, near0 = lax.optimization_barrier((message2, near0))
    near2 = lax.ppermute(message2, "gx", chips)
    message3, near1 = lax.optimization_barrier((message3, near1))
    near3 = lax.ppermute(message3, "gx", chips)
    extra = pltpu.VMEM((2, full, lanes), jnp.float32)
    out, state = call(
        functools.partial(third_kernel, n_halo),
        [f32(planes, rows, lanes), f32(4, full, lanes)],
        [VMEM] * 9,
        [ANY, VMEM],
        [extra, extra, pltpu.VMEM((full, lanes), jnp.float32), pltpu.VMEM((2, ROWS, lanes), jnp.float32),
         pltpu.VMEM((2, rows, lanes), jnp.float32), pltpu.SemaphoreType.DMA((2,))],
        cells=11 * plane,
    )(u0, u1, margin, kappa, velocity, rate, near0, near1, beside)
    out, base, gain = call(
        fourth_kernel,
        [f32(planes, rows, lanes), f32(rows, lanes), f32(rows, lanes)],
        [VMEM] * 6 + [ANY],
        [ANY, VMEM, VMEM],
        [pltpu.VMEM((full, lanes), jnp.float32), pltpu.VMEM((rows, lanes), jnp.float32), pltpu.SemaphoreType.DMA],
        {6: 0},
        cells=3 * plane,
    )(state, margin, kappa, velocity, rate, near2, out)
    return call(
        last_kernel,
        f32(planes, rows, lanes),
        [VMEM] * 3 + [ANY],
        ANY,
        [pltpu.VMEM((rows, lanes), jnp.float32), pltpu.SemaphoreType.DMA],
        {3: 0},
        cells=plane // 8,
    )(base, gain, near3, out)


def solution(mesh):
    placed = P("gx", "gy", None)
    return jax.shard_map(local, mesh=mesh, in_specs=(placed,) * 4, out_specs=placed, check_vma=False)
```

```python
import functools

import jax
import jax.numpy as jnp
from jax import lax
from jax.experimental import pallas as pl
from jax.experimental.pallas import tpu as pltpu
from jax.sharding import PartitionSpec as P

robin_p = 0.6
own = (1.0 - robin_p / 2) / (1.0 + robin_p / 2)
far = ((1.0 - own) + robin_p * (1.0 + own) / 2) / (1.0 + robin_p / 2)

VMEM = pl.BlockSpec(memory_space=pltpu.VMEM)
ANY = pl.BlockSpec(memory_space=pl.ANY)
HBM = pl.BlockSpec(memory_space=pltpu.HBM)
HALO = 4
ROWS = 8
LANES = 128


def parity(axis):
    return lax.rem(lax.axis_index(axis), 2)


def plane_at(d, odd):
    return d + odd * (3 - 2 * d)


def pick(odd, yes, no):
    return jnp.where(jnp.broadcast_to(odd == 1, yes.shape), yes, no)


def load(ref, index, tile):
    rows = pl.ds(tile * ROWS if isinstance(tile, int) else pl.multiple_of(tile * ROWS, ROWS), ROWS)
    return [ref[*index, rows, k : k + LANES] for k in range(0, ref.shape[-1], LANES)]


def store(ref, index, tile, pieces):
    rows = pl.ds(tile * ROWS if isinstance(tile, int) else pl.multiple_of(tile * ROWS, ROWS), ROWS)
    for k, piece in enumerate(pieces):
        ref[*index, rows, k * LANES : (k + 1) * LANES] = piece


def ghost(mine, received=None):
    if received is None:
        return [m * own for m in mine]
    return [r * far + m * own for r, m in zip(received, mine)]


def updated(odd, cur, before, after, toward, away, kappa, velocity, rate):
    row = lax.broadcasted_iota(jnp.int32, (ROWS, LANES), 0)
    lane = lax.broadcasted_iota(jnp.int32, (ROWS, LANES), 1)
    zero = jnp.zeros((ROWS, LANES), jnp.float32)
    out = []
    for k, c in enumerate(cur):
        up = pltpu.roll(jnp.where(row == ROWS - 1, before[k], c), 1, 0)
        down = pltpu.roll(jnp.where(row == 0, after[k], c), ROWS - 1, 0)
        low = cur[k - 1] if k else zero
        high = cur[k + 1] if k + 1 < len(cur) else zero
        left = pltpu.roll(jnp.where(lane == LANES - 1, low, c), 1, 1)
        right = pltpu.roll(jnp.where(lane == 0, high, c), LANES - 1, 1)
        minus_x = pick(odd, away[k], toward[k]) if toward is not None else away[k]
        lap = away[k] + toward[k]
        lap = lap + up + down
        lap = lap + left + right
        lap = lap - 6.0 * c
        square = c * c
        bottom = 1.0 + square
        inverse = pl.reciprocal(bottom, approx=True)
        inverse = inverse * (2.0 - bottom * inverse)
        react = rate[k] * c * (square * inverse)
        out.append(c + kappa[k] * lap - velocity[k] * (c - minus_x) - react)
    return out


def sweep(odd, wanted, source, coefs, margins, near, distant, sink, inner, edges, unroll):
    needed = sorted({e for d in wanted for e in (d - 1, d, d + 1) if 0 <= e <= 3})
    last = source(wanted[0])[0].shape[-2] // ROWS - 1

    def body(tile):
        if isinstance(tile, int):
            before, after = (tile or last + 1) - 1, (tile + 1) % (last + 1)
        elif inner[0] > 0:
            before, after = tile - 1, tile + 1
        else:
            before, after = lax.select(tile == 0, last, tile - 1), tile + 1
        refs, at = (margins, 0) if isinstance(tile, int) and tile == last else (coefs, tile)
        state = {d: load(*source(d), tile) for d in needed}
        for d in wanted:
            cur = state[d]
            toward = state[d - 1] if d > 0 else ghost(cur, near(tile))
            away = state[d + 1] if d < 3 else ghost(cur, distant(tile))
            p = plane_at(d, odd)
            kvr = [load(ref, (*lead, p), at) for ref, lead in refs]
            sink(d, tile, updated(odd, cur, load(*source(d), before), load(*source(d), after), toward, away, *kvr))

    def loop(tile, carry):
        body(tile)
        return carry

    if inner[1] > inner[0]:
        lax.fori_loop(inner[0], inner[1], loop, 0, unroll=unroll)
    for tile in edges:
        body(tile)


def coefficients(margin, kappa, velocity, rate):
    return [(ref, ()) for ref in (kappa, velocity, rate)], [(margin, (i,)) for i in range(3)]


def none(tile):
    return None


def pack_kernel(n_halo, initial, kappa, velocity, rate, plane, *rest):
    halos, (tiles, sems) = rest[:n_halo], rest[n_halo:]
    odd_x, odd_y = parity("gx"), parity("gy")
    rows = initial.shape[1]
    copies = [pltpu.make_async_copy(initial.at[plane_at(0, odd_x)], plane, sems.at[0])]
    for f, field in enumerate((initial, kappa, velocity, rate)):
        copies.append(pltpu.make_async_copy(field.at[:, :ROWS, :], tiles.at[f, 0], sems.at[1 + 2 * f]))
        copies.append(pltpu.make_async_copy(field.at[:, rows - ROWS :, :], tiles.at[f, 1], sems.at[2 + 2 * f]))
    for copy in copies:
        copy.start()
    for copy in copies[1:]:
        copy.wait()
    for f in range(4):
        first, last = tiles[f, 0, :, :HALO], tiles[f, 1, :, ROWS - HALO :]
        halos[0][4 * f : 4 * f + 4] = pick(odd_y, first, last)
        if n_halo > 1:
            halos[1][4 * f : 4 * f + 4] = pick(odd_y, last, first)
    copies[0].wait()


def load_kernel(initial, kappa, velocity, rate, u0, u1, kappa_v, velocity_v, rate_v, sems):
    odd = parity("gx")
    planes, rows = initial.shape[:2]
    own_rows = pl.ds(0, rows)
    fields = [(initial, u0), (kappa, kappa_v), (velocity, velocity_v), (rate, rate_v)]
    copies = {}
    for d in range(planes):
        p = plane_at(d, odd)
        copies[0, d] = pltpu.make_async_copy(initial.at[p], u0.at[p, own_rows], sems.at[0, d])
    for d in range(planes):
        p = plane_at(d, odd)
        for f in range(1, 4):
            copies[f, d] = pltpu.make_async_copy(fields[f][0].at[p], fields[f][1].at[p], sems.at[f, d])
    for copy in copies.values():
        copy.start()
    for d in range(planes):
        copies[0, d].wait()

    def sink(d, tile, pieces):
        store(u1, (plane_at(d, odd),), tile, pieces)

    coefs = [(ref, ()) for ref in (kappa_v, velocity_v, rate_v)]
    tiles = rows // ROWS
    for d in range(planes):
        for f in range(1, 4):
            copies[f, d].wait()
        sweep(odd, [d], lambda e: (u0, (plane_at(e, odd),)), coefs, None, none, none, sink,
              (1, tiles - 1), (), 7 if (tiles - 2) % 7 == 0 else 1)


def first_kernel(n_halo, u0_in, u1_in, kappa, velocity, rate, *rest):
    del u0_in, u1_in
    halos, (u0, u1, margin, message) = rest[:n_halo], rest[n_halo:]
    odd, odd_y = parity("gx"), parity("gy")
    rows = kappa.shape[1]
    for f in range(4):
        one = halos[0][4 * f : 4 * f + 4]
        two = halos[1][4 * f : 4 * f + 4] if n_halo > 1 else jnp.zeros_like(one)
        edge = jnp.concatenate([pick(odd_y, two, one), pick(odd_y, one, two)], axis=1)
        if f == 0:
            u0[:, rows:, :] = edge
        else:
            margin[f - 1] = edge

    def sink(d, tile, pieces):
        store(u1, (plane_at(d, odd),), tile, pieces)

    tiles = rows // ROWS
    sweep(odd, [0, 1, 2, 3], lambda d: (u0, (plane_at(d, odd),)), *coefficients(margin, kappa, velocity, rate),
          none, none, sink, (0, 0), (0, tiles - 1, tiles), 1)
    p = plane_at(0, odd)
    message[:rows] = u1[p, :rows]
    zero = u0[p, rows:]
    one = u1[p, rows:]
    if n_halo > 1:
        message[rows : rows + ROWS] = zero
        message[rows + ROWS :] = one
    else:
        half = lax.broadcasted_iota(jnp.int32, zero.shape, 0) // HALO
        message[rows:] = jnp.where(half == odd_y, zero, pltpu.roll(one, HALO, 0))


def second_kernel(u0, u1, margin, kappa, velocity, rate, message2, message3, beside, u2):
    odd = parity("gx")
    rows = kappa.shape[1]
    coefs, margins = coefficients(margin, kappa, velocity, rate)
    tiles = rows // ROWS

    def sink2(d, tile, pieces):
        store(u2, (plane_at(d, odd),), tile, pieces)
        if d == 0:
            store(message2, (), tile, pieces)
        if d == 3:
            store(beside, (2,), tile, pieces)

    def sink3(d, tile, pieces):
        if d == 0:
            store(message3, (), tile, pieces)
        if d == 3:
            store(beside, (3,), tile, pieces)

    sweep(odd, [0, 1, 2, 3], lambda d: (u1, (plane_at(d, odd),)), coefs, margins, none, none, sink2,
          (0, tiles), (tiles,), 4)
    sweep(odd, [0, 3], lambda d: (u2, (plane_at(d, odd),)), coefs, margins, none, none, sink3, (0, tiles), (), 4)
    beside[3, rows:] = jnp.zeros(beside[3, rows:].shape, jnp.float32)
    beside[0] = u0[plane_at(3, odd)]
    beside[1] = u1[plane_at(3, odd)]


def near_kernel(n_halo, u0, u1, margin, kappa, velocity, rate, near0, near1, state, v1, edges):
    odd = parity("gx")
    rows = kappa.shape[1]
    coefs, margins = coefficients(margin, kappa, velocity, rate)
    tiles = rows // ROWS
    if n_halo > 1:
        edges[0] = near1[rows : rows + ROWS]
        edges[1] = near1[rows + ROWS :]
    else:
        edges[0] = near1[rows:]
        edges[1] = pltpu.roll(near1[rows:], HALO, 0)

    def near(step, ref):
        return lambda tile: load(edges, (step,), 0) if isinstance(tile, int) and tile == tiles else load(ref, (), tile)

    def sink1(d, tile, pieces):
        store(v1, (), tile, pieces)

    def sink2(d, tile, pieces):
        store(state, (d,), tile, pieces)

    def source1(d):
        return (v1, ()) if d == 0 else (u1, (plane_at(d, odd),))

    sweep(odd, [0], lambda d: (u0, (plane_at(d, odd),)), coefs, margins, near(0, near0), none, sink1,
          (0, tiles), (tiles,), 4)
    sweep(odd, [0, 1], source1, coefs, margins, near(1, near1), none, sink2, (0, tiles), (tiles,), 4)


def third_kernel(u0, u1, margin, kappa, velocity, rate, begun, beside, out, state, v1, v2, v3, done, sems):
    odd = parity("gx")
    rows = kappa.shape[1]
    coefs, margins = coefficients(margin, kappa, velocity, rate)
    tiles = rows // ROWS

    def distant(step):
        return lambda tile: load(beside, (step,), tile)

    def sink1(d, tile, pieces):
        store(v1, (), tile, pieces)

    def source1(d):
        return (v1, ()) if d == 3 else (u1, (plane_at(d, odd),))

    def sink2(d, tile, pieces):
        store(v2, (d - 2,), tile, pieces)

    def source2(d):
        return (begun, (d,)) if d < 2 else (v2, (d - 2,))

    def sink3(d, tile, pieces):
        if d < 3:
            store(state, (d - 1,), tile, pieces)
        else:
            store(v3, (), tile, pieces)

    def source3(d):
        return (state, (d - 1,)) if d < 3 else (v3, ())

    def sink4(d, tile, pieces):
        store(done, (d - 2,), tile, pieces)

    whole = ((0, tiles), (tiles,), 4)
    sweep(odd, [3], lambda d: (u0, (plane_at(d, odd),)), coefs, margins, none, distant(0), sink1, *whole)
    sweep(odd, [2, 3], source1, coefs, margins, none, distant(1), sink2, *whole)
    sweep(odd, [1, 2, 3], source2, coefs, margins, none, distant(2), sink3, *whole)
    sweep(odd, [2, 3], source3, coefs, margins, none, distant(3), sink4, (0, tiles), (), 4)
    copies = [pltpu.make_async_copy(done.at[d - 2], out.at[plane_at(d, odd)], sems.at[d - 2]) for d in (2, 3)]
    for copy in copies:
        copy.start()
    for copy in copies:
        copy.wait()


def fourth_kernel(begun, state, margin, kappa, velocity, rate, near2, out_in, out, base, gain, v3, done, sem):
    del out_in
    odd = parity("gx")
    rows = kappa.shape[1]
    coefs, margins = coefficients(margin, kappa, velocity, rate)
    tiles = rows // ROWS

    def sink3(d, tile, pieces):
        store(v3, (), tile, pieces)

    sweep(odd, [0], lambda d: (begun, (d,)), coefs, margins, lambda tile: load(near2, (), tile), none, sink3,
          (0, tiles), (tiles,), 4)

    def source3(d):
        return (v3, ()) if d == 0 else (state, (d - 1,))

    def sink4(d, tile, pieces):
        store(done if d else base, (), tile, pieces)

    sweep(odd, [0, 1], source3, coefs, margins, none, none, sink4, (0, tiles), (), 4)
    copy = pltpu.make_async_copy(done, out.at[plane_at(1, odd)], sem)
    copy.start()
    p = plane_at(0, odd)

    def gains(tile, carry):
        both = zip(load(kappa, (p,), tile), load(velocity, (p,), tile))
        store(gain, (), tile, [far * (k + pick(odd, jnp.zeros_like(v), v)) for k, v in both])
        return carry

    lax.fori_loop(0, tiles, gains, 0)
    copy.wait()


def last_kernel(base, gain, near3, out_in, out, done, sem):
    del out_in
    odd = parity("gx")
    done[...] = base[...] + gain[...] * near3[...]
    copy = pltpu.make_async_copy(done, out.at[plane_at(0, odd)], sem)
    copy.start()
    copy.wait()


def pairs(count, first, wrap):
    out = []
    for i in range(first, count, 2):
        if i + 1 < count or wrap:
            out += [(i, (i + 1) % count), ((i + 1) % count, i)]
    return out


def f32(*shape):
    return jax.ShapeDtypeStruct(shape, jnp.float32)


def call(kernel, out_shape, in_specs, out_specs, scratch=(), aliases=None, weight=0, limit=12):
    return pl.pallas_call(
        kernel,
        out_shape=out_shape,
        in_specs=in_specs,
        out_specs=out_specs,
        scratch_shapes=scratch,
        input_output_aliases=aliases or {},
        cost_estimate=pl.CostEstimate(flops=int(weight * 1e9), bytes_accessed=int(weight * 3.0e6), transcendentals=0),
        compiler_params=pltpu.CompilerParams(vmem_limit_bytes=limit * 1024 * 1024),
    )


def local(initial, kappa, velocity, rate):
    planes, rows, lanes = initial.shape
    full = rows + ROWS
    count_y = lax.axis_size("gy")
    count_x = lax.axis_size("gx")
    n_halo = 1 if count_y == 2 else 2
    chips = pairs(count_x, 1, True)
    cores = pairs(count_x, 0, False)
    rows_pairs = [pairs(count_y, 0, False), pairs(count_y, 1, False)][:n_halo]
    block, wide = f32(planes, rows, lanes), f32(planes, full, lanes)
    wide_plane = pltpu.VMEM((full, lanes), jnp.float32)

    plane0, *halos = call(
        functools.partial(pack_kernel, n_halo),
        [f32(rows, lanes)] + [f32(16, HALO, lanes)] * n_halo,
        [HBM] * 4,
        [ANY] + [VMEM] * n_halo,
        [pltpu.VMEM((4, 2, planes, ROWS, lanes), jnp.float32), pltpu.SemaphoreType.DMA((9,))],
        weight=1,
    )(*[pltpu.with_memory_space_constraint(x, pltpu.HBM) for x in (initial, kappa, velocity, rate)])
    near0 = lax.ppermute(plane0, "gx", chips)
    halos = [lax.ppermute(halo, "gy", which) for halo, which in zip(halos, rows_pairs)]
    u0, u1, *coefs = call(
        load_kernel,
        [wide, wide, block, block, block],
        [HBM] * 4,
        [VMEM] * 5,
        [pltpu.SemaphoreType.DMA((4, planes))],
        weight=20,
    )(*[pltpu.with_memory_space_constraint(x, pltpu.HBM) for x in (initial, kappa, velocity, rate)])
    u0, u1, margin, message1 = call(
        functools.partial(first_kernel, n_halo),
        [wide, wide, f32(3, planes, ROWS, lanes), f32(rows + ROWS * n_halo, lanes)],
        [VMEM] * (5 + n_halo),
        [VMEM] * 4,
        aliases={0: 0, 1: 1},
        weight=1,
    )(u0, u1, *coefs, *halos)
    near1 = lax.ppermute(message1, "gx", chips)
    u1, near0 = lax.optimization_barrier((u1, near0))
    message2, message3, beside = call(
        second_kernel,
        [f32(full, lanes), f32(rows, lanes), f32(4, full, lanes)],
        [VMEM] * 6,
        [VMEM] * 3,
        [pltpu.VMEM((planes, full, lanes), jnp.float32)],
        weight=20,
    )(u0, u1, margin, *coefs)
    near2 = lax.ppermute(message2, "gx", chips)
    beside = lax.ppermute(beside, "gx", cores)
    message3, near1 = lax.optimization_barrier((message3, near1))
    near3 = lax.ppermute(message3, "gx", chips)
    begun = call(
        functools.partial(near_kernel, n_halo),
        f32(2, full, lanes),
        [VMEM] * 8,
        VMEM,
        [wide_plane, pltpu.VMEM((2, ROWS, lanes), jnp.float32)],
        weight=20,
    )(u0, u1, margin, *coefs, near0, near1)
    out, state = call(
        third_kernel,
        [block, f32(2, full, lanes)],
        [VMEM] * 8,
        [ANY, VMEM],
        [wide_plane, pltpu.VMEM((2, full, lanes), jnp.float32), wide_plane,
         pltpu.VMEM((2, rows, lanes), jnp.float32), pltpu.SemaphoreType.DMA((2,))],
        weight=20,
    )(u0, u1, margin, *coefs, begun, beside)
    out, base, gain = call(
        fourth_kernel,
        [block, f32(rows, lanes), f32(rows, lanes)],
        [VMEM] * 7 + [ANY],
        [ANY, VMEM, VMEM],
        [wide_plane, pltpu.VMEM((rows, lanes), jnp.float32), pltpu.SemaphoreType.DMA],
        {7: 0},
        weight=20,
    )(begun, state, margin, *coefs, near2, out)
    return call(
        last_kernel,
        block,
        [VMEM] * 3 + [ANY],
        ANY,
        [pltpu.VMEM((rows, lanes), jnp.float32), pltpu.SemaphoreType.DMA],
        {3: 0},
        weight=1,
    )(base, gain, near3, out)


def solution(mesh):
    placed = P("gx", "gy", None)
    return jax.shard_map(local, mesh=mesh, in_specs=(placed,) * 4, out_specs=placed, check_vma=False)
```

```python
import functools

import jax
import jax.numpy as jnp
from jax import lax
from jax.experimental import pallas as pl
from jax.experimental.pallas import tpu as pltpu
from jax.sharding import PartitionSpec as P

robin_p = 0.6
own = (1.0 - robin_p / 2) / (1.0 + robin_p / 2)
far = ((1.0 - own) + robin_p * (1.0 + own) / 2) / (1.0 + robin_p / 2)

VMEM = pl.BlockSpec(memory_space=pltpu.VMEM)
ANY = pl.BlockSpec(memory_space=pl.ANY)
HBM = pl.BlockSpec(memory_space=pltpu.HBM)
HALO = 4
WEIGHTS = (1, 20, 1, 60, 20, 1, 1, 1, 1)
ROWS = 8
LANES = 128
UNROLL = 4


def parity(axis):
    return lax.rem(lax.axis_index(axis), 2)


def plane_at(d, odd):
    return d + odd * (3 - 2 * d)


def pick(odd, yes, no):
    return jnp.where(jnp.broadcast_to(odd == 1, yes.shape), yes, no)


def load(ref, index, tile):
    rows = pl.ds(tile * ROWS if isinstance(tile, int) else pl.multiple_of(tile * ROWS, ROWS), ROWS)
    return [ref[*index, rows, k : k + LANES] for k in range(0, ref.shape[-1], LANES)]


def store(ref, index, tile, pieces):
    rows = pl.ds(tile * ROWS if isinstance(tile, int) else pl.multiple_of(tile * ROWS, ROWS), ROWS)
    for k, piece in enumerate(pieces):
        ref[*index, rows, k * LANES : (k + 1) * LANES] = piece


def ghost(mine, received=None):
    if received is None:
        return [m * own for m in mine]
    return [r * far + m * own for r, m in zip(received, mine)]


def updated(odd, cur, before, after, toward, away, kappa, velocity, rate):
    row = lax.broadcasted_iota(jnp.int32, (ROWS, LANES), 0)
    lane = lax.broadcasted_iota(jnp.int32, (ROWS, LANES), 1)
    zero = jnp.zeros((ROWS, LANES), jnp.float32)
    out = []
    for k, c in enumerate(cur):
        up = pltpu.roll(jnp.where(row == ROWS - 1, before[k], c), 1, 0)
        down = pltpu.roll(jnp.where(row == 0, after[k], c), ROWS - 1, 0)
        low = cur[k - 1] if k else zero
        high = cur[k + 1] if k + 1 < len(cur) else zero
        left = pltpu.roll(jnp.where(lane == LANES - 1, low, c), 1, 1)
        right = pltpu.roll(jnp.where(lane == 0, high, c), LANES - 1, 1)
        minus_x = pick(odd, away[k], toward[k]) if toward is not None else away[k]
        lap = away[k] + toward[k]
        lap = lap + up + down
        lap = lap + left + right
        lap = lap - 6.0 * c
        square = c * c
        bottom = 1.0 + square
        inverse = pl.reciprocal(bottom, approx=True)
        inverse = inverse * (2.0 - bottom * inverse)
        react = rate[k] * c * (square * inverse)
        out.append(c + kappa[k] * lap - velocity[k] * (c - minus_x) - react)
    return out


def sweep(odd, wanted, source, coefs, margins, near, distant, sink, inner, edges, unroll):
    needed = sorted({e for d in wanted for e in (d - 1, d, d + 1) if 0 <= e <= 3})
    last = source(wanted[0])[0].shape[-2] // ROWS - 1

    def body(tile):
        if isinstance(tile, int):
            before, after = (tile or last + 1) - 1, (tile + 1) % (last + 1)
        elif inner[0] > 0:
            before, after = tile - 1, tile + 1
        else:
            before, after = lax.select(tile == 0, last, tile - 1), tile + 1
        refs, at = (margins, 0) if isinstance(tile, int) and tile == last else (coefs, tile)
        state = {d: load(*source(d), tile) for d in needed}
        for d in wanted:
            cur = state[d]
            toward = state[d - 1] if d > 0 else ghost(cur, near(tile))
            away = state[d + 1] if d < 3 else ghost(cur, distant(tile))
            p = plane_at(d, odd)
            kvr = [load(ref, (*lead, p), at) for ref, lead in refs]
            sink(d, tile, updated(odd, cur, load(*source(d), before), load(*source(d), after), toward, away, *kvr))

    def loop(tile, carry):
        body(tile)
        return carry

    if inner[1] > inner[0]:
        lax.fori_loop(inner[0], inner[1], loop, 0, unroll=unroll)
    for tile in edges:
        body(tile)


def coefficients(margin, kappa, velocity, rate):
    return [(ref, ()) for ref in (kappa, velocity, rate)], [(margin, (i,)) for i in range(3)]


def none(tile):
    return None


def pack_kernel(n_halo, initial, kappa, velocity, rate, plane, *rest):
    halos, (tiles, sems) = rest[:n_halo], rest[n_halo:]
    odd_x, odd_y = parity("gx"), parity("gy")
    rows = initial.shape[1]
    copies = [pltpu.make_async_copy(initial.at[plane_at(0, odd_x)], plane, sems.at[0])]
    for f, field in enumerate((initial, kappa, velocity, rate)):
        copies.append(pltpu.make_async_copy(field.at[:, :ROWS, :], tiles.at[f, 0], sems.at[1 + 2 * f]))
        copies.append(pltpu.make_async_copy(field.at[:, rows - ROWS :, :], tiles.at[f, 1], sems.at[2 + 2 * f]))
    for copy in copies[1:] + copies[:1]:
        copy.start()
    for f in range(4):
        copies[1 + 2 * f].wait()
        copies[2 + 2 * f].wait()
        first, last = tiles[f, 0, :, :HALO], tiles[f, 1, :, ROWS - HALO :]
        halos[0][4 * f : 4 * f + 4] = pick(odd_y, first, last)
        if n_halo > 1:
            halos[1][4 * f : 4 * f + 4] = pick(odd_y, last, first)
    copies[0].wait()


def load_kernel(initial, kappa, velocity, rate, u0, u1, kappa_v, velocity_v, rate_v, sems):
    odd = parity("gx")
    planes, rows = initial.shape[:2]
    own_rows = pl.ds(0, rows)
    fields = [(kappa, kappa_v), (velocity, velocity_v), (rate, rate_v)]
    copies = {}
    for d in range(planes):
        p = plane_at(d, odd)
        copies[0, d] = pltpu.make_async_copy(initial.at[p], u0.at[p, own_rows], sems.at[0, d])
    for d in range(planes):
        p = plane_at(d, odd)
        for f, (field, held) in enumerate(fields):
            copies[f + 1, d] = pltpu.make_async_copy(field.at[p], held.at[p], sems.at[f + 1, d])
    for copy in copies.values():
        copy.start()
    for d in range(planes):
        copies[0, d].wait()

    def sink(d, tile, pieces):
        store(u1, (plane_at(d, odd),), tile, pieces)

    coefs = [(ref, ()) for ref in (kappa_v, velocity_v, rate_v)]
    tiles = rows // ROWS
    for d in range(planes):
        for f in range(1, 4):
            copies[f, d].wait()
        sweep(odd, [d], lambda e: (u0, (plane_at(e, odd),)), coefs, None, none, none, sink,
              (1, tiles - 1), (), 7 if tiles % 7 == 2 else 1)


def first_kernel(n_halo, u0_in, u1_in, kappa, velocity, rate, *rest):
    del u0_in, u1_in
    halos, (u0, u1, margin, message) = rest[:n_halo], rest[n_halo:]
    odd, odd_y = parity("gx"), parity("gy")
    rows = kappa.shape[1]
    for f in range(4):
        one = halos[0][4 * f : 4 * f + 4]
        two = halos[1][4 * f : 4 * f + 4] if n_halo > 1 else jnp.zeros_like(one)
        edge = jnp.concatenate([pick(odd_y, two, one), pick(odd_y, one, two)], axis=1)
        if f == 0:
            u0[:, rows:, :] = edge
        else:
            margin[f - 1] = edge

    def sink(d, tile, pieces):
        store(u1, (plane_at(d, odd),), tile, pieces)

    tiles = rows // ROWS
    sweep(odd, [0, 1, 2, 3], lambda d: (u0, (plane_at(d, odd),)), *coefficients(margin, kappa, velocity, rate),
          none, none, sink, (0, 0), (0, tiles - 1, tiles), 1)
    p = plane_at(0, odd)
    message[:rows] = u1[p, :rows]
    zero = u0[p, rows:]
    one = u1[p, rows:]
    if n_halo > 1:
        message[rows : rows + ROWS] = zero
        message[rows + ROWS :] = one
    else:
        half = lax.broadcasted_iota(jnp.int32, zero.shape, 0) // HALO
        message[rows:] = jnp.where(half == odd_y, zero, pltpu.roll(one, HALO, 0))


def second_kernel(u0, u1, margin, kappa, velocity, rate, message2, message3, beside, u2):
    odd = parity("gx")
    rows = kappa.shape[1]
    coefs, margins = coefficients(margin, kappa, velocity, rate)
    tiles = rows // ROWS

    def sink2(d, tile, pieces):
        store(u2, (plane_at(d, odd),), tile, pieces)
        if d == 0:
            store(message2, (), tile, pieces)
        if d == 3:
            store(beside, (2,), tile, pieces)

    def sink3(d, tile, pieces):
        if d == 0:
            store(message3, (), tile, pieces)
        if d == 3:
            store(beside, (3,), tile, pieces)

    sweep(odd, [0, 1, 2, 3], lambda d: (u1, (plane_at(d, odd),)), coefs, margins, none, none, sink2,
          (0, tiles), (tiles,), UNROLL)
    sweep(odd, [0, 3], lambda d: (u2, (plane_at(d, odd),)), coefs, margins, none, none, sink3, (0, tiles), (), UNROLL)
    beside[3, rows:] = jnp.zeros(beside[3, rows:].shape, jnp.float32)
    beside[0] = u0[plane_at(3, odd)]
    beside[1] = u1[plane_at(3, odd)]


def gain_kernel(kappa, velocity, gain):
    odd = parity("gx")
    p = plane_at(0, odd)

    def body(tile, carry):
        both = zip(load(kappa, (p,), tile), load(velocity, (p,), tile))
        store(gain, (), tile, [far * (k + pick(odd, jnp.zeros_like(v), v)) for k, v in both])
        return carry

    lax.fori_loop(0, kappa.shape[1] // ROWS, body, 0, unroll=UNROLL)


STATE = {(2, 2): 0, (2, 3): 1, (3, 3): 2}
MORE = {(2, 0): 0, (2, 1): 1, (3, 1): 2, (3, 2): 3}


def stages(odd, u0, u1, state, more, others):
    def at(step, d):
        if (step, d) in others:
            return others[step, d]
        if (step, d) in STATE:
            return state, (STATE[step, d],)
        if (step, d) in MORE:
            return more, (MORE[step, d],)
        return (u0, u1)[step], (plane_at(d, odd),)

    def sink(step):
        def put(d, tile, pieces):
            ref, index = at(step, d)
            store(ref, index, tile, pieces)

        return put

    return lambda step: functools.partial(at, step), sink


def far_kernel(u0, u1, margin, kappa, velocity, rate, beside, state, v1):
    odd = parity("gx")
    tiles = kappa.shape[1] // ROWS
    coefs, margins = coefficients(margin, kappa, velocity, rate)
    source, sink = stages(odd, u0, u1, state, None, {(1, 3): (v1, ())})
    whole = ((0, tiles), (tiles,), UNROLL)

    def distant(step):
        return lambda tile: load(beside, (step,), tile)

    sweep(odd, [3], source(0), coefs, margins, none, distant(0), sink(1), *whole)
    sweep(odd, [2, 3], source(1), coefs, margins, none, distant(1), sink(2), *whole)
    sweep(odd, [3], source(2), coefs, margins, none, distant(2), sink(3), *whole)


def near_kernel(n_halo, u0, u1, margin, kappa, velocity, rate, near0, near1, beside, state, out, more, almost,
                v1, edges, done, sem):
    odd = parity("gx")
    rows = kappa.shape[1]
    coefs, margins = coefficients(margin, kappa, velocity, rate)
    tiles = rows // ROWS
    if n_halo > 1:
        edges[0] = near1[rows : rows + ROWS]
        edges[1] = near1[rows + ROWS :]
    else:
        edges[0] = near1[rows:]
        edges[1] = pltpu.roll(near1[rows:], HALO, 0)
    source, sink = stages(odd, u0, u1, state, more, {(1, 0): (v1, ())})
    whole = ((0, tiles), (tiles,), UNROLL)

    def near(step, ref):
        return lambda tile: load(edges, (step,), 0) if isinstance(tile, int) and tile == tiles else load(ref, (), tile)

    def distant(tile):
        return load(beside, (3,), tile)

    def finish(d, tile, pieces):
        store(done if d == 3 else almost, (), tile, pieces)

    sweep(odd, [0], source(0), coefs, margins, near(0, near0), none, sink(1), *whole)
    sweep(odd, [0, 1], source(1), coefs, margins, near(1, near1), none, sink(2), *whole)
    sweep(odd, [1, 2], source(2), coefs, margins, none, none, sink(3), *whole)
    sweep(odd, [2, 3], source(3), coefs, margins, none, distant, finish, (0, tiles), (), UNROLL)
    copy = pltpu.make_async_copy(done, out.at[plane_at(3, odd)], sem)
    copy.start()
    copy.wait()


def fourth_kernel(more, almost, margin, kappa, velocity, rate, near2, out_in, out, base, v3, done, sems):
    del out_in
    odd = parity("gx")
    tiles = kappa.shape[1] // ROWS
    coefs, margins = coefficients(margin, kappa, velocity, rate)
    copies = [pltpu.make_async_copy(almost, out.at[plane_at(2, odd)], sems.at[0]),
              pltpu.make_async_copy(done, out.at[plane_at(1, odd)], sems.at[1])]
    copies[0].start()
    source, sink = stages(odd, None, None, None, more, {(3, 0): (v3, ())})

    def finish(d, tile, pieces):
        store(done if d else base, (), tile, pieces)

    sweep(odd, [0], source(2), coefs, margins, lambda tile: load(near2, (), tile), none, sink(3),
          (0, tiles), (tiles,), UNROLL)
    sweep(odd, [0, 1], source(3), coefs, margins, none, none, finish, (0, tiles), (), UNROLL)
    copies[1].start()
    for copy in copies:
        copy.wait()


def last_kernel(base, gain, near3, out_in, out, done, sems):
    del out_in
    odd = parity("gx")
    rows = base.shape[0]
    part = rows // 4
    copies = []
    for i in range(4):
        span = pl.ds(i * part, part)
        done[span] = base[span] + gain[span] * near3[span]
        copies.append(pltpu.make_async_copy(done.at[span], out.at[plane_at(0, odd), span], sems.at[i]))
        copies[-1].start()
    for copy in copies:
        copy.wait()


def pairs(count, first, wrap):
    out = []
    for i in range(first, count, 2):
        if i + 1 < count or wrap:
            out += [(i, (i + 1) % count), ((i + 1) % count, i)]
    return out


def f32(*shape):
    return jax.ShapeDtypeStruct(shape, jnp.float32)


def call(kernel, out_shape, in_specs, out_specs, scratch=(), aliases=None, weight=0, limit=12):
    return pl.pallas_call(
        kernel,
        out_shape=out_shape,
        in_specs=in_specs,
        out_specs=out_specs,
        scratch_shapes=scratch,
        input_output_aliases=aliases or {},
        cost_estimate=pl.CostEstimate(flops=int(weight * 1e9), bytes_accessed=int(weight * 3.0e6), transcendentals=0),
        compiler_params=pltpu.CompilerParams(vmem_limit_bytes=limit * 1024 * 1024),
    )


def local(initial, kappa, velocity, rate):
    planes, rows, lanes = initial.shape
    full = rows + ROWS
    count_y = lax.axis_size("gy")
    count_x = lax.axis_size("gx")
    n_halo = 1 if count_y == 2 else 2
    chips = pairs(count_x, 1, True)
    cores = pairs(count_x, 0, False)
    rows_pairs = [pairs(count_y, 0, False), pairs(count_y, 1, False)][:n_halo]
    block, wide, plane, wide_plane = f32(planes, rows, lanes), f32(planes, full, lanes), f32(rows, lanes), f32(full, lanes)

    def scratch(*shape):
        return pltpu.VMEM(shape, jnp.float32)

    fields = [pltpu.with_memory_space_constraint(x, pltpu.HBM) for x in (initial, kappa, velocity, rate)]
    message0, *halos = call(
        functools.partial(pack_kernel, n_halo),
        [plane] + [f32(16, HALO, lanes)] * n_halo,
        [HBM] * 4,
        [ANY] + [VMEM] * n_halo,
        [scratch(4, 2, planes, ROWS, lanes), pltpu.SemaphoreType.DMA((9,))],
        weight=WEIGHTS[0],
    )(*fields)
    near0 = lax.ppermute(message0, "gx", chips)
    halos = [lax.ppermute(halo, "gy", which) for halo, which in zip(halos, rows_pairs)]
    u0, u1, *coefs = call(
        load_kernel,
        [wide, wide, block, block, block],
        [HBM] * 4,
        [VMEM] * 5,
        [pltpu.SemaphoreType.DMA((4, planes))],
        weight=WEIGHTS[1],
    )(*fields)
    u0, u1, margin, message1 = call(
        functools.partial(first_kernel, n_halo),
        [wide, wide, f32(3, planes, ROWS, lanes), f32(rows + ROWS * n_halo, lanes)],
        [VMEM] * (5 + n_halo),
        [VMEM] * 4,
        aliases={0: 0, 1: 1},
        weight=WEIGHTS[2],
    )(u0, u1, *coefs, *halos)
    near1 = lax.ppermute(message1, "gx", chips)
    message2, message3, beside = call(
        second_kernel,
        [wide_plane, plane, f32(4, full, lanes)],
        [VMEM] * 6,
        [VMEM] * 3,
        [scratch(planes, full, lanes)],
        weight=WEIGHTS[3],
    )(u0, u1, margin, *coefs)
    beside = lax.ppermute(beside, "gx", cores)
    near2 = lax.ppermute(message2, "gx", chips)
    near3 = lax.ppermute(message3, "gx", chips)
    gain = call(gain_kernel, plane, [VMEM] * 2, VMEM, weight=WEIGHTS[4])(*coefs[:2])
    beside, gain = lax.optimization_barrier((beside, gain))
    state = call(
        far_kernel,
        f32(3, full, lanes),
        [VMEM] * 7,
        VMEM,
        [scratch(full, lanes)],
        weight=WEIGHTS[5],
    )(u0, u1, margin, *coefs, beside)
    out, more, almost = call(
        functools.partial(near_kernel, n_halo),
        [block, f32(4, full, lanes), plane],
        [VMEM] * 10,
        [ANY, VMEM, VMEM],
        [scratch(full, lanes), scratch(2, ROWS, lanes), scratch(rows, lanes), pltpu.SemaphoreType.DMA],
        weight=WEIGHTS[6],
    )(u0, u1, margin, *coefs, near0, near1, beside, state)
    out, base = call(
        fourth_kernel,
        [block, plane],
        [VMEM] * 7 + [ANY],
        [ANY, VMEM],
        [scratch(full, lanes), scratch(rows, lanes), pltpu.SemaphoreType.DMA((2,))],
        {7: 0},
        weight=WEIGHTS[7],
    )(more, almost, margin, *coefs, near2, out)
    return call(
        last_kernel,
        block,
        [VMEM] * 3 + [ANY],
        ANY,
        [scratch(rows, lanes), pltpu.SemaphoreType.DMA((4,))],
        {3: 0},
        weight=WEIGHTS[8],
    )(base, gain, near3, out)


def solution(mesh):
    placed = P("gx", "gy", None)
    return jax.shard_map(local, mesh=mesh, in_specs=(placed,) * 4, out_specs=placed, check_vma=False)
```

```python
import functools

import jax
import jax.numpy as jnp
from jax import lax
from jax.experimental import pallas as pl
from jax.experimental.pallas import tpu as pltpu
from jax.sharding import PartitionSpec as P

robin_p = 0.6
own = (1.0 - robin_p / 2) / (1.0 + robin_p / 2)
far = ((1.0 - own) + robin_p * (1.0 + own) / 2) / (1.0 + robin_p / 2)

VMEM = pl.BlockSpec(memory_space=pltpu.VMEM)
ANY = pl.BlockSpec(memory_space=pl.ANY)
HBM = pl.BlockSpec(memory_space=pltpu.HBM)
HALO = 4
WEIGHTS = (1, 1, 20, 1, 60, 20, 1, 1, 1, 1)
ROWS = 8
LANES = 128
PARTS = 4
UNROLL = 4
GROUPS = (8, 8, 4, 4)
UNROLLS = (1, 1, 1, 1)


def parity(axis):
    return lax.rem(lax.axis_index(axis), 2)


def plane_at(d, odd):
    return d + odd * (3 - 2 * d)


def pick(odd, yes, no):
    return jnp.where(jnp.broadcast_to(odd == 1, yes.shape), yes, no)


def load(ref, index, tile):
    rows = pl.ds(tile * ROWS if isinstance(tile, int) else pl.multiple_of(tile * ROWS, ROWS), ROWS)
    return [ref[*index, rows, k : k + LANES] for k in range(0, ref.shape[-1], LANES)]


def store(ref, index, tile, pieces):
    rows = pl.ds(tile * ROWS if isinstance(tile, int) else pl.multiple_of(tile * ROWS, ROWS), ROWS)
    for k, piece in enumerate(pieces):
        ref[*index, rows, k * LANES : (k + 1) * LANES] = piece


def ghost(mine, received=None):
    if received is None:
        return [m * own for m in mine]
    return [r * far + m * own for r, m in zip(received, mine)]


def updated(odd, cur, before, after, toward, away, kappa, velocity, rate):
    row = lax.broadcasted_iota(jnp.int32, (ROWS, LANES), 0)
    lane = lax.broadcasted_iota(jnp.int32, (ROWS, LANES), 1)
    zero = jnp.zeros((ROWS, LANES), jnp.float32)
    out = []
    for k, c in enumerate(cur):
        up = pltpu.roll(jnp.where(row == ROWS - 1, before[k], c), 1, 0)
        down = pltpu.roll(jnp.where(row == 0, after[k], c), ROWS - 1, 0)
        low = cur[k - 1] if k else zero
        high = cur[k + 1] if k + 1 < len(cur) else zero
        left = pltpu.roll(jnp.where(lane == LANES - 1, low, c), 1, 1)
        right = pltpu.roll(jnp.where(lane == 0, high, c), LANES - 1, 1)
        minus_x = pick(odd, away[k], toward[k]) if toward is not None else away[k]
        lap = away[k] + toward[k]
        lap = lap + up + down
        lap = lap + left + right
        lap = lap - 6.0 * c
        square = c * c
        bottom = 1.0 + square
        inverse = pl.reciprocal(bottom, approx=True)
        inverse = inverse * (2.0 - bottom * inverse)
        react = rate[k] * c * (square * inverse)
        out.append(c + kappa[k] * lap - velocity[k] * (c - minus_x) - react)
    return out


def sweep(odd, wanted, source, coefs, margins, near, distant, sink, inner, edges=()):
    needed = sorted({e for d in wanted for e in (d - 1, d, d + 1) if 0 <= e <= 3})
    last = source(wanted[0])[0].shape[-2] // ROWS - 1

    def work(tiles, together):
        state = {(d, i): load(*source(d), tile) for i, tile in enumerate(tiles) for d in needed}
        results = []
        for i, tile in enumerate(tiles):
            if isinstance(tile, int):
                before, after = (tile or last + 1) - 1, (tile + 1) % (last + 1)
            else:
                before, after = tile - 1, tile + 1
                if inner[0] == 0 and i == 0:
                    before = lax.select(tile == 0, last, before)
            refs, at = (margins, 0) if isinstance(tile, int) and tile == last else (coefs, tile)
            for d in wanted:
                cur = state[d, i]
                toward = state[d - 1, i] if d > 0 else ghost(cur, near(tile))
                away = state[d + 1, i] if d < 3 else ghost(cur, distant(tile))
                upper = state[d, i - 1] if together and i > 0 else load(*source(d), before)
                lower = state[d, i + 1] if together and i + 1 < len(tiles) else load(*source(d), after)
                p = plane_at(d, odd)
                kvr = [load(ref, (*lead, p), at) for ref, lead in refs]
                results.append((d, tile, updated(odd, cur, upper, lower, toward, away, *kvr)))
        for d, tile, pieces in results:
            sink(d, tile, pieces)

    count = inner[1] - inner[0]
    if count:
        size = max(n for n in range(1, GROUPS[len(wanted) - 1] + 1) if count % n == 0)

        def loop(index, carry):
            work([inner[0] + index * size + i for i in range(size)], True)
            return carry

        lax.fori_loop(0, count // size, loop, 0, unroll=UNROLLS[len(wanted) - 1])
    if edges:
        work(list(edges), False)


def coefficients(margin, kappa, velocity, rate):
    return [(ref, ()) for ref in (kappa, velocity, rate)], [(margin, (i,)) for i in range(3)]


def none(tile):
    return None


def plane_kernel(initial, plane, sems):
    p = plane_at(0, parity("gx"))
    part = plane.shape[0] // PARTS
    spans = [pl.ds(i * part, part) for i in range(PARTS)]
    copies = [pltpu.make_async_copy(initial.at[p, span], plane.at[span], sems.at[i]) for i, span in enumerate(spans)]
    for copy in copies:
        copy.start()
    for copy in copies:
        copy.wait()


def load_kernel(n_halo, initial, kappa, velocity, rate, u0, u1, kappa_v, velocity_v, rate_v, message, *rest):
    halos, (tiles, sems) = rest[:n_halo], rest[n_halo:]
    odd, odd_y = parity("gx"), parity("gy")
    rows = initial.shape[1]
    own_rows = pl.ds(0, rows)
    near, next_to = plane_at(0, odd), plane_at(1, odd)
    fields = (initial, kappa, velocity, rate)
    copies = [pltpu.make_async_copy(initial.at[p], u0.at[p, own_rows], sems.at[i]) for i, p in enumerate((near, next_to))]
    for f, held in enumerate((kappa_v, velocity_v, rate_v)):
        copies.append(pltpu.make_async_copy(fields[f + 1].at[near], held.at[near], sems.at[2 + f]))
    packs = []
    for f, field in enumerate(fields):
        packs.append(pltpu.make_async_copy(field.at[:, :ROWS, :], tiles.at[f, 0], sems.at[5 + 2 * f]))
        packs.append(pltpu.make_async_copy(field.at[:, rows - ROWS :, :], tiles.at[f, 1], sems.at[6 + 2 * f]))
    for copy in copies + packs:
        copy.start()
    u0[:, rows:, :] = jnp.zeros(u0[:, rows:, :].shape, jnp.float32)
    for copy in copies:
        copy.wait()

    def sink(d, tile, pieces):
        store(u1, (plane_at(d, odd),), tile, pieces)
        store(message, (), tile, pieces)

    coefs = [(ref, ()) for ref in (kappa_v, velocity_v, rate_v)]
    sweep(odd, [0], lambda d: (u0, (plane_at(d, odd),)), coefs, None, none, none, sink, (0, rows // ROWS))
    for copy in packs:
        copy.wait()
    for f in range(4):
        first, last = tiles[f, 0, :, :HALO], tiles[f, 1, :, ROWS - HALO :]
        halos[0][4 * f : 4 * f + 4] = pick(odd_y, first, last)
        if n_halo > 1:
            halos[1][4 * f : 4 * f + 4] = pick(odd_y, last, first)


def inner_kernel(initial, kappa, velocity, rate, u0_in, u1_in, kappa_in, velocity_in, rate_in,
                 u0, u1, kappa_v, velocity_v, rate_v, sems):
    del u0_in, u1_in, kappa_in, velocity_in, rate_in
    odd = parity("gx")
    planes, rows = initial.shape[:2]
    own_rows = pl.ds(0, rows)
    copies = {}
    for d in range(2, planes):
        p = plane_at(d, odd)
        copies[0, d] = pltpu.make_async_copy(initial.at[p], u0.at[p, own_rows], sems.at[0, d])
    for d in range(1, planes):
        p = plane_at(d, odd)
        for f, (field, held) in enumerate([(kappa, kappa_v), (velocity, velocity_v), (rate, rate_v)]):
            copies[f + 1, d] = pltpu.make_async_copy(field.at[p], held.at[p], sems.at[f + 1, d])
    order = [(0, 2), (1, 1), (2, 1), (3, 1), (0, 3)] + [(f, d) for d in range(2, planes) for f in range(1, 4)]
    for key in order:
        copies[key].start()

    def sink(d, tile, pieces):
        store(u1, (plane_at(d, odd),), tile, pieces)

    coefs = [(ref, ()) for ref in (kappa_v, velocity_v, rate_v)]
    for d in range(1, planes):
        if (0, d + 1) in copies:
            copies[0, d + 1].wait()
        for f in range(1, 4):
            copies[f, d].wait()
        sweep(odd, [d], lambda e: (u0, (plane_at(e, odd),)), coefs, None, none, none, sink, (0, rows // ROWS))


def first_kernel(n_halo, u0_in, u1_in, kappa, velocity, rate, *rest):
    del u0_in, u1_in
    halos, (u0, u1, margin, tail) = rest[:n_halo], rest[n_halo:]
    odd, odd_y = parity("gx"), parity("gy")
    rows = kappa.shape[1]
    for f in range(4):
        one = halos[0][4 * f : 4 * f + 4]
        two = halos[1][4 * f : 4 * f + 4] if n_halo > 1 else jnp.zeros_like(one)
        edge = jnp.concatenate([pick(odd_y, two, one), pick(odd_y, one, two)], axis=1)
        if f == 0:
            u0[:, rows:, :] = edge
        else:
            margin[f - 1] = edge

    def sink(d, tile, pieces):
        store(u1, (plane_at(d, odd),), tile, pieces)

    tiles = rows // ROWS
    sweep(odd, [0, 1, 2, 3], lambda d: (u0, (plane_at(d, odd),)), *coefficients(margin, kappa, velocity, rate),
          none, none, sink, (0, 0), (0, tiles - 1, tiles))
    p = plane_at(0, odd)
    row = lax.broadcasted_iota(jnp.int32, (ROWS, u0.shape[2]), 0)
    before = u0[p, rows:]
    before = jnp.where(row == HALO - 1, pltpu.roll(u1[p, rows - ROWS : rows], HALO, 0), before)
    tail[...] = jnp.where(row == HALO, pltpu.roll(u1[p, :ROWS], HALO, 0), before)


def packed(odd_y, n_halo, zero, one, two):
    row = lax.broadcasted_iota(jnp.int32, zero.shape, 0)
    rest = jnp.where(row == 2, pltpu.roll(two, 2, 0), jnp.where(row == 5, pltpu.roll(two, ROWS - 2, 0), one))
    if n_halo > 1:
        return [zero, rest]
    return [jnp.where(row // HALO == odd_y, zero, pltpu.roll(rest, HALO, 0))]


def unpacked(n_halo, tiles):
    zero, rest = tiles if n_halo > 1 else (tiles[0], pltpu.roll(tiles[0], HALO, 0))
    row = lax.broadcasted_iota(jnp.int32, zero.shape, 0)
    two = jnp.where(row < HALO, pltpu.roll(rest, ROWS - 2, 0), pltpu.roll(rest, 2, 0))
    return zero, rest, two


def second_kernel(n_halo, u0, u1, margin, tail, kappa, velocity, rate, message2, message3, beside, u2):
    odd, odd_y = parity("gx"), parity("gy")
    rows = kappa.shape[1]
    coefs, margins = coefficients(margin, kappa, velocity, rate)
    tiles = rows // ROWS

    def sink2(d, tile, pieces):
        store(u2, (plane_at(d, odd),), tile, pieces)
        if d == 0 and not (isinstance(tile, int) and tile == tiles):
            store(message2, (), tile, pieces)
        if d == 3:
            store(beside, (2,), tile, pieces)

    def sink3(d, tile, pieces):
        if d == 0:
            store(message3, (), tile, pieces)
        if d == 3:
            store(beside, (3,), tile, pieces)

    sweep(odd, [0, 1, 2, 3], lambda d: (u1, (plane_at(d, odd),)), coefs, margins, none, none, sink2, (0, tiles), (tiles,))
    p = plane_at(0, odd)
    for i, part in enumerate(packed(odd_y, n_halo, tail[...], u1[p, rows:], u2[p, rows:])):
        message2[rows + i * ROWS : rows + (i + 1) * ROWS] = part
    sweep(odd, [0, 3], lambda d: (u2, (plane_at(d, odd),)), coefs, margins, none, none, sink3, (0, tiles))
    beside[3, rows:] = jnp.zeros(beside[3, rows:].shape, jnp.float32)
    beside[0] = u0[plane_at(3, odd)]
    beside[1] = u1[plane_at(3, odd)]


def gain_kernel(kappa, velocity, gain):
    odd = parity("gx")
    p = plane_at(0, odd)

    def body(tile, carry):
        both = zip(load(kappa, (p,), tile), load(velocity, (p,), tile))
        store(gain, (), tile, [far * (k + pick(odd, jnp.zeros_like(v), v)) for k, v in both])
        return carry

    lax.fori_loop(0, kappa.shape[1] // ROWS, body, 0, unroll=UNROLL)


STATE = {(1, 0): 0, (2, 1): 1, (2, 2): 2, (3, 2): 3, (3, 3): 4, (2, 3): 5}
MORE = {(2, 0): 0, (3, 1): 1}


def stages(odd, u0, u1, state, more, others):
    def at(step, d):
        if (step, d) in others:
            return others[step, d]
        if (step, d) in STATE:
            return state, (STATE[step, d],)
        if (step, d) in MORE:
            return more, (MORE[step, d],)
        return (u0, u1)[step], (plane_at(d, odd),)

    def sink(step):
        def put(d, tile, pieces):
            ref, index = at(step, d)
            store(ref, index, tile, pieces)

        return put

    return lambda step: functools.partial(at, step), sink


def far_kernel(u0, u1, margin, kappa, velocity, rate, near0, beside, state, final3, v1):
    odd = parity("gx")
    tiles = kappa.shape[1] // ROWS
    coefs, margins = coefficients(margin, kappa, velocity, rate)
    source, sink = stages(odd, u0, u1, state, None, {(1, 3): (v1, ())})
    own_rows, edge = (0, tiles), ((0, 0), (tiles,))

    def near(tile):
        return load(near0, (), tile)

    def distant(step):
        return lambda tile: load(beside, (step,), tile)

    def finish(d, tile, pieces):
        store(final3, (), tile, pieces)

    sweep(odd, [0, 3], source(0), coefs, margins, near, distant(0), sink(1), own_rows)
    sweep(odd, [3], source(0), coefs, margins, none, distant(0), sink(1), *edge)
    sweep(odd, [1, 2, 3], source(1), coefs, margins, none, distant(1), sink(2), own_rows)
    sweep(odd, [2, 3], source(1), coefs, margins, none, distant(1), sink(2), *edge)
    sweep(odd, [2, 3], source(2), coefs, margins, none, distant(2), sink(3), own_rows)
    sweep(odd, [3], source(2), coefs, margins, none, distant(2), sink(3), *edge)
    sweep(odd, [3], source(3), coefs, margins, none, distant(3), finish, own_rows)


def near_kernel(kappa, velocity, rate, u1, near1, state, final3, out, more, final2, sem):
    odd = parity("gx")
    copy = pltpu.make_async_copy(final3, out.at[plane_at(3, odd)], sem)
    copy.start()
    own_rows = (0, kappa.shape[1] // ROWS)
    coefs, margins = coefficients(None, kappa, velocity, rate)
    source, sink = stages(odd, None, u1, state, more, {})

    def near(tile):
        return load(near1, (), tile)

    def finish(d, tile, pieces):
        store(final2, (), tile, pieces)

    sweep(odd, [0], source(1), coefs, margins, near, none, sink(2), own_rows)
    sweep(odd, [1], source(2), coefs, margins, none, none, sink(3), own_rows)
    sweep(odd, [2], source(3), coefs, margins, none, none, finish, own_rows)
    copy.wait()


def fourth_kernel(n_halo, margin, kappa, velocity, rate, u0, u1, near1, near2, state_in, more_in, final2_in, out_in,
                  state, more, final2, out, base, v3, edges, final1, sems):
    del state_in, more_in, final2_in, out_in
    odd, odd_y = parity("gx"), parity("gy")
    rows, lanes = kappa.shape[1:]
    tiles = rows // ROWS
    coefs, margins = coefficients(margin, kappa, velocity, rate)
    zero, one, two = unpacked(n_halo, [near2[rows + i * ROWS : rows + (i + 1) * ROWS] for i in range(n_halo)])
    row = lax.broadcasted_iota(jnp.int32, (ROWS, lanes), 0)
    top, bottom = row == 0, row == ROWS - 1
    if n_halo == 1:
        top, bottom = jnp.logical_and(top, odd_y == 1), jnp.logical_and(bottom, odd_y == 0)
    outer = pltpu.roll(zero, HALO, 0)
    edges[0] = zero
    edges[1] = one
    edges[2] = two
    edges[3] = jnp.where(top, outer, near1[:ROWS])
    edges[4] = jnp.where(bottom, outer, near1[rows - ROWS :])
    source, sink = stages(odd, u0, u1, state, more, {(3, 0): (v3, ())})
    copies = [pltpu.make_async_copy(final2, out.at[plane_at(2, odd)], sems.at[0]),
              pltpu.make_async_copy(final1, out.at[plane_at(1, odd)], sems.at[1])]

    def near(step):
        def piece(tile):
            if step == 1 and isinstance(tile, int) and tile < tiles:
                return load(edges, (4 if tile else 3,), 0)
            if isinstance(tile, int) and tile == tiles:
                return load(edges, (step,), 0)
            return load(near2, (), tile)

        return piece

    def finish(d, tile, pieces):
        store({0: base, 1: final1, 2: final2}[d], (), tile, pieces)

    own_rows, margin_only, outer_tiles = (0, tiles), ((0, 0), (tiles,)), ((0, 0), (0, tiles - 1, tiles))
    sweep(odd, [0], source(0), coefs, margins, near(0), none, sink(1), *margin_only)
    sweep(odd, [0], source(1), coefs, margins, near(1), none, sink(2), *outer_tiles)
    sweep(odd, [1], source(1), coefs, margins, none, none, sink(2), *margin_only)
    sweep(odd, [1], source(2), coefs, margins, none, none, sink(3), *outer_tiles)
    sweep(odd, [2], source(2), coefs, margins, none, none, sink(3), *margin_only)
    sweep(odd, [2], source(3), coefs, margins, none, none, finish, (0, 0), (0, tiles - 1))
    copies[0].start()
    sweep(odd, [0], source(2), coefs, margins, near(2), none, sink(3), own_rows, (tiles,))
    sweep(odd, [1], source(3), coefs, margins, none, none, finish, own_rows)
    copies[1].start()
    sweep(odd, [0], source(3), coefs, margins, none, none, finish, own_rows)
    for copy in copies:
        copy.wait()


def last_kernel(base, gain, near3, out_in, out, done, sems):
    del out_in
    odd = parity("gx")
    rows = base.shape[0]
    part = rows // PARTS
    copies = []
    for i in range(PARTS):
        span = pl.ds(i * part, part)
        done[span] = base[span] + gain[span] * near3[span]
        copies.append(pltpu.make_async_copy(done.at[span], out.at[plane_at(0, odd), span], sems.at[i]))
        copies[-1].start()
    for copy in copies:
        copy.wait()


def pairs(count, first, wrap):
    out = []
    for i in range(first, count, 2):
        if i + 1 < count or wrap:
            out += [(i, (i + 1) % count), ((i + 1) % count, i)]
    return out


def f32(*shape):
    return jax.ShapeDtypeStruct(shape, jnp.float32)


def call(kernel, out_shape, in_specs, out_specs, scratch=(), aliases=None, weight=0, limit=12):
    return pl.pallas_call(
        kernel,
        out_shape=out_shape,
        in_specs=in_specs,
        out_specs=out_specs,
        scratch_shapes=scratch,
        input_output_aliases=aliases or {},
        cost_estimate=pl.CostEstimate(flops=int(weight * 1e9), bytes_accessed=int(weight * 3.0e6), transcendentals=0),
        compiler_params=pltpu.CompilerParams(vmem_limit_bytes=limit * 1024 * 1024),
    )


def local(initial, kappa, velocity, rate):
    planes, rows, lanes = initial.shape
    full = rows + ROWS
    count_y = lax.axis_size("gy")
    count_x = lax.axis_size("gx")
    n_halo = 1 if count_y == 2 else 2
    chips = pairs(count_x, 1, True)
    cores = pairs(count_x, 0, False)
    rows_pairs = [pairs(count_y, 0, False), pairs(count_y, 1, False)][:n_halo]
    block, wide, plane, wide_plane = f32(planes, rows, lanes), f32(planes, full, lanes), f32(rows, lanes), f32(full, lanes)

    def scratch(*shape):
        return pltpu.VMEM(shape, jnp.float32)

    fields = [pltpu.with_memory_space_constraint(x, pltpu.HBM) for x in (initial, kappa, velocity, rate)]
    message0 = call(plane_kernel, plane, [HBM], ANY, [pltpu.SemaphoreType.DMA((PARTS,))], weight=WEIGHTS[0])(fields[0])
    near0 = lax.ppermute(message0, "gx", chips)
    fields[0], message0 = lax.optimization_barrier((fields[0], message0))
    u0, u1, *rest = call(
        functools.partial(load_kernel, n_halo),
        [wide, wide, block, block, block, plane] + [f32(16, HALO, lanes)] * n_halo,
        [HBM] * 4,
        [VMEM] * (6 + n_halo),
        [scratch(4, 2, planes, ROWS, lanes), pltpu.SemaphoreType.DMA((13,))],
        weight=WEIGHTS[1],
    )(*fields)
    coefs, message1, halos = rest[:3], rest[3], rest[4:]
    halos = [lax.ppermute(halo, "gy", which) for halo, which in zip(halos, rows_pairs)]
    near1 = lax.ppermute(message1, "gx", chips)
    u0, u1, *coefs = call(
        inner_kernel,
        [wide, wide, block, block, block],
        [HBM] * 4 + [VMEM] * 5,
        [VMEM] * 5,
        [pltpu.SemaphoreType.DMA((4, planes))],
        {4: 0, 5: 1, 6: 2, 7: 3, 8: 4},
        weight=WEIGHTS[2],
    )(*fields, u0, u1, *coefs)
    u0, u1, margin, tail = call(
        functools.partial(first_kernel, n_halo),
        [wide, wide, f32(3, planes, ROWS, lanes), f32(ROWS, lanes)],
        [VMEM] * (5 + n_halo),
        [VMEM] * 4,
        aliases={0: 0, 1: 1},
        weight=WEIGHTS[3],
    )(u0, u1, *coefs, *halos)
    message2, message3, beside = call(
        functools.partial(second_kernel, n_halo),
        [f32(rows + ROWS * n_halo, lanes), plane, f32(4, full, lanes)],
        [VMEM] * 7,
        [VMEM] * 3,
        [scratch(planes, full, lanes)],
        weight=WEIGHTS[4],
    )(u0, u1, margin, tail, *coefs)
    beside = lax.ppermute(beside, "gx", cores)
    near2 = lax.ppermute(message2, "gx", chips)
    near3 = lax.ppermute(message3, "gx", chips)
    gain = call(gain_kernel, plane, [VMEM] * 2, VMEM, weight=WEIGHTS[5])(*coefs[:2])
    beside, gain = lax.optimization_barrier((beside, gain))
    state, final3 = call(
        far_kernel,
        [f32(len(STATE), full, lanes), plane],
        [VMEM] * 8,
        [VMEM] * 2,
        [scratch(full, lanes)],
        weight=WEIGHTS[6],
    )(u0, u1, margin, *coefs, near0, beside)
    out, more, final2 = call(
        near_kernel,
        [block, f32(2, full, lanes), plane],
        [VMEM] * 7,
        [ANY, VMEM, VMEM],
        [pltpu.SemaphoreType.DMA],
        weight=WEIGHTS[7],
    )(*coefs, u1, near1, state, final3)
    state, more, final2, out, base = call(
        functools.partial(fourth_kernel, n_halo),
        [f32(len(STATE), full, lanes), f32(2, full, lanes), plane, block, plane],
        [VMEM] * 11 + [ANY],
        [VMEM] * 3 + [ANY, VMEM],
        [scratch(full, lanes), scratch(5, ROWS, lanes), scratch(rows, lanes), pltpu.SemaphoreType.DMA((2,))],
        {8: 0, 9: 1, 10: 2, 11: 3},
        weight=WEIGHTS[8],
    )(margin, *coefs, u0, u1, near1, near2, state, more, final2, out)
    return call(
        last_kernel,
        block,
        [VMEM] * 3 + [ANY],
        ANY,
        [scratch(rows, lanes), pltpu.SemaphoreType.DMA((PARTS,))],
        {3: 0},
        weight=WEIGHTS[9],
    )(base, gain, near3, out)


def solution(mesh):
    placed = P("gx", "gy", None)
    return jax.shard_map(local, mesh=mesh, in_specs=(placed,) * 4, out_specs=placed, check_vma=False)
```

```python
import functools

import jax
import jax.numpy as jnp
from jax import lax
from jax.experimental import pallas as pl
from jax.experimental.pallas import tpu as pltpu
from jax.sharding import PartitionSpec as P

robin_p = 0.6
own = (1.0 - robin_p / 2) / (1.0 + robin_p / 2)
far = ((1.0 - own) + robin_p * (1.0 + own) / 2) / (1.0 + robin_p / 2)

VMEM = pl.BlockSpec(memory_space=pltpu.VMEM)
ANY = pl.BlockSpec(memory_space=pl.ANY)
HBM = pl.BlockSpec(memory_space=pltpu.HBM)
HALO = 4
WEIGHTS = (1, 1, 20, 1, 60, 20, 0, 0, 0, 0)
ROWS = 8
LANES = 128
PARTS = 4
UNROLL = 4
GROUPS = (8, 8, 4, 4)


def parity(axis):
    return lax.rem(lax.axis_index(axis), 2)


def plane_at(d, odd):
    return d + odd * (3 - 2 * d)


def pick(odd, yes, no):
    return jnp.where(jnp.broadcast_to(odd == 1, yes.shape), yes, no)


def load(ref, index, tile):
    rows = pl.ds(tile * ROWS if isinstance(tile, int) else pl.multiple_of(tile * ROWS, ROWS), ROWS)
    return [ref[*index, rows, k : k + LANES] for k in range(0, ref.shape[-1], LANES)]


def store(ref, index, tile, pieces):
    rows = pl.ds(tile * ROWS if isinstance(tile, int) else pl.multiple_of(tile * ROWS, ROWS), ROWS)
    for k, piece in enumerate(pieces):
        ref[*index, rows, k * LANES : (k + 1) * LANES] = piece


def ghost(mine, received=None):
    if received is None:
        return [m * own for m in mine]
    return [r * far + m * own for r, m in zip(received, mine)]


def updated(odd, cur, before, after, toward, away, kappa, velocity, rate):
    row = lax.broadcasted_iota(jnp.int32, (ROWS, LANES), 0)
    lane = lax.broadcasted_iota(jnp.int32, (ROWS, LANES), 1)
    zero = jnp.zeros((ROWS, LANES), jnp.float32)
    out = []
    for k, c in enumerate(cur):
        up = pltpu.roll(jnp.where(row == ROWS - 1, before[k], c), 1, 0)
        down = pltpu.roll(jnp.where(row == 0, after[k], c), ROWS - 1, 0)
        low = cur[k - 1] if k else zero
        high = cur[k + 1] if k + 1 < len(cur) else zero
        left = pltpu.roll(jnp.where(lane == LANES - 1, low, c), 1, 1)
        right = pltpu.roll(jnp.where(lane == 0, high, c), LANES - 1, 1)
        minus_x = pick(odd, away[k], toward[k]) if toward is not None else away[k]
        lap = away[k] + toward[k]
        lap = lap + up + down
        lap = lap + left + right
        lap = lap - 6.0 * c
        square = c * c
        bottom = 1.0 + square
        inverse = pl.reciprocal(bottom, approx=True)
        inverse = inverse * (2.0 - bottom * inverse)
        react = rate[k] * c * (square * inverse)
        out.append(c + kappa[k] * lap - velocity[k] * (c - minus_x) - react)
    return out


def sweep(odd, wanted, source, coefs, margins, near, distant, sink, inner, edges=()):
    needed = sorted({e for d in wanted for e in (d - 1, d, d + 1) if 0 <= e <= 3})
    last = source(wanted[0])[0].shape[-2] // ROWS - 1

    def work(tiles, together):
        state = {(d, i): load(*source(d), tile) for i, tile in enumerate(tiles) for d in needed}
        results = []
        for i, tile in enumerate(tiles):
            if isinstance(tile, int):
                before, after = (tile or last + 1) - 1, (tile + 1) % (last + 1)
            else:
                before, after = tile - 1, tile + 1
                if inner[0] == 0 and i == 0:
                    before = lax.select(tile == 0, last, before)
            refs, at = (margins, 0) if isinstance(tile, int) and tile == last else (coefs, tile)
            for d in wanted:
                cur = state[d, i]
                toward = state[d - 1, i] if d > 0 else ghost(cur, near(tile))
                away = state[d + 1, i] if d < 3 else ghost(cur, distant(tile))
                upper = state[d, i - 1] if together and i > 0 else load(*source(d), before)
                lower = state[d, i + 1] if together and i + 1 < len(tiles) else load(*source(d), after)
                p = plane_at(d, odd)
                kvr = [load(ref, (*lead, p), at) for ref, lead in refs]
                results.append((d, tile, updated(odd, cur, upper, lower, toward, away, *kvr)))
        for d, tile, pieces in results:
            sink(d, tile, pieces)

    count = inner[1] - inner[0]
    if count:
        size = max(n for n in range(1, GROUPS[len(wanted) - 1] + 1) if count % n == 0)

        def loop(index, carry):
            work([inner[0] + index * size + i for i in range(size)], True)
            return carry

        lax.fori_loop(0, count // size, loop, 0)
    if edges:
        work(list(edges), False)


def coefficients(margin, kappa, velocity, rate):
    return [(ref, ()) for ref in (kappa, velocity, rate)], [(margin, (i,)) for i in range(3)]


def none(tile):
    return None


def plane_kernel(initial, plane, sems):
    p = plane_at(0, parity("gx"))
    part = plane.shape[0] // PARTS
    spans = [pl.ds(i * part, part) for i in range(PARTS)]
    copies = [pltpu.make_async_copy(initial.at[p, span], plane.at[span], sems.at[i]) for i, span in enumerate(spans)]
    for copy in copies:
        copy.start()
    for copy in copies:
        copy.wait()


def load_kernel(n_halo, initial, kappa, velocity, rate, u0, u1, kappa_v, velocity_v, rate_v, message, *rest):
    halos, (tiles, sems) = rest[:n_halo], rest[n_halo:]
    odd, odd_y = parity("gx"), parity("gy")
    rows = initial.shape[1]
    own_rows = pl.ds(0, rows)
    near, next_to = plane_at(0, odd), plane_at(1, odd)
    fields = (initial, kappa, velocity, rate)
    copies = [pltpu.make_async_copy(initial.at[p], u0.at[p, own_rows], sems.at[i]) for i, p in enumerate((near, next_to))]
    for f, held in enumerate((kappa_v, velocity_v, rate_v)):
        copies.append(pltpu.make_async_copy(fields[f + 1].at[near], held.at[near], sems.at[2 + f]))
    packs = []
    for f, field in enumerate(fields):
        packs.append(pltpu.make_async_copy(field.at[:, :ROWS, :], tiles.at[f, 0], sems.at[5 + 2 * f]))
        packs.append(pltpu.make_async_copy(field.at[:, rows - ROWS :, :], tiles.at[f, 1], sems.at[6 + 2 * f]))
    for copy in copies + packs:
        copy.start()
    u0[:, rows:, :] = jnp.zeros(u0[:, rows:, :].shape, jnp.float32)
    for copy in copies:
        copy.wait()

    def sink(d, tile, pieces):
        store(u1, (plane_at(d, odd),), tile, pieces)
        store(message, (), tile, pieces)

    coefs = [(ref, ()) for ref in (kappa_v, velocity_v, rate_v)]
    sweep(odd, [0], lambda d: (u0, (plane_at(d, odd),)), coefs, None, none, none, sink, (0, rows // ROWS))
    for copy in packs:
        copy.wait()
    for f in range(4):
        first, last = tiles[f, 0, :, :HALO], tiles[f, 1, :, ROWS - HALO :]
        halos[0][4 * f : 4 * f + 4] = pick(odd_y, first, last)
        if n_halo > 1:
            halos[1][4 * f : 4 * f + 4] = pick(odd_y, last, first)


def inner_kernel(initial, kappa, velocity, rate, u0_in, u1_in, kappa_in, velocity_in, rate_in,
                 u0, u1, kappa_v, velocity_v, rate_v, u2, sems):
    del u0_in, u1_in, kappa_in, velocity_in, rate_in
    odd = parity("gx")
    planes, rows = initial.shape[:2]
    own_rows = pl.ds(0, rows)
    copies = {}
    for d in range(2, planes):
        p = plane_at(d, odd)
        copies[0, d] = pltpu.make_async_copy(initial.at[p], u0.at[p, own_rows], sems.at[0, d])
    for d in range(1, planes):
        p = plane_at(d, odd)
        for f, (field, held) in enumerate([(kappa, kappa_v), (velocity, velocity_v), (rate, rate_v)]):
            copies[f + 1, d] = pltpu.make_async_copy(field.at[p], held.at[p], sems.at[f + 1, d])
    order = [(0, 2), (1, 1), (2, 1), (3, 1), (0, 3)] + [(f, d) for d in range(2, planes) for f in range(1, 4)]
    for key in order:
        copies[key].start()

    def sink(d, tile, pieces):
        store(u1, (plane_at(d, odd),), tile, pieces)

    coefs = [(ref, ()) for ref in (kappa_v, velocity_v, rate_v)]
    for d in range(1, planes):
        if (0, d + 1) in copies:
            copies[0, d + 1].wait()
        for f in range(1, 4):
            copies[f, d].wait()
        sweep(odd, [d], lambda e: (u0, (plane_at(e, odd),)), coefs, None, none, none, sink, (0, rows // ROWS))

    def sink2(d, tile, pieces):
        store(u2, (plane_at(d, odd),), tile, pieces)

    sweep(odd, [0, 1, 2, 3], lambda d: (u1, (plane_at(d, odd),)), coefs, None, none, none, sink2, (1, rows // ROWS - 1))


def first_kernel(n_halo, u0_in, u1_in, u2_in, kappa, velocity, rate, *rest):
    del u0_in, u1_in, u2_in
    halos, (u0, u1, u2, margin, message) = rest[:n_halo], rest[n_halo:]
    odd, odd_y = parity("gx"), parity("gy")
    rows = kappa.shape[1]
    for f in range(4):
        one = halos[0][4 * f : 4 * f + 4]
        two = halos[1][4 * f : 4 * f + 4] if n_halo > 1 else jnp.zeros_like(one)
        edge = jnp.concatenate([pick(odd_y, two, one), pick(odd_y, one, two)], axis=1)
        if f == 0:
            u0[:, rows:, :] = edge
        else:
            margin[f - 1] = edge

    def sink(d, tile, pieces):
        store(u1, (plane_at(d, odd),), tile, pieces)

    def sink2(d, tile, pieces):
        store(u2, (plane_at(d, odd),), tile, pieces)

    tiles = rows // ROWS
    outer, every = ((0, 0), (0, tiles - 1, tiles)), [0, 1, 2, 3]
    coefs, margins = coefficients(margin, kappa, velocity, rate)
    sweep(odd, every, lambda d: (u0, (plane_at(d, odd),)), coefs, margins, none, none, sink, *outer)
    sweep(odd, every, lambda d: (u1, (plane_at(d, odd),)), coefs, margins, none, none, sink2, *outer)
    p = plane_at(0, odd)
    row = lax.broadcasted_iota(jnp.int32, (ROWS, u0.shape[2]), 0)
    before = u0[p, rows:]
    before = jnp.where(row == HALO - 1, pltpu.roll(u1[p, rows - ROWS : rows], HALO, 0), before)
    before = jnp.where(row == HALO, pltpu.roll(u1[p, :ROWS], HALO, 0), before)
    message[:rows] = u2[p, :rows]
    for i, part in enumerate(packed(odd_y, n_halo, before, u1[p, rows:], u2[p, rows:])):
        message[rows + i * ROWS : rows + (i + 1) * ROWS] = part


def packed(odd_y, n_halo, zero, one, two):
    row = lax.broadcasted_iota(jnp.int32, zero.shape, 0)
    rest = jnp.where(row == 2, pltpu.roll(two, 2, 0), jnp.where(row == 5, pltpu.roll(two, ROWS - 2, 0), one))
    if n_halo > 1:
        return [zero, rest]
    return [jnp.where(row // HALO == odd_y, zero, pltpu.roll(rest, HALO, 0))]


def unpacked(n_halo, tiles):
    zero, rest = tiles if n_halo > 1 else (tiles[0], pltpu.roll(tiles[0], HALO, 0))
    row = lax.broadcasted_iota(jnp.int32, zero.shape, 0)
    two = jnp.where(row < HALO, pltpu.roll(rest, ROWS - 2, 0), pltpu.roll(rest, 2, 0))
    return zero, rest, two


def second_kernel(u0, u1, u2, margin, kappa, velocity, rate, message3, beside):
    odd = parity("gx")
    rows = kappa.shape[1]
    coefs, margins = coefficients(margin, kappa, velocity, rate)

    def sink(d, tile, pieces):
        if d == 0:
            store(message3, (), tile, pieces)
        else:
            store(beside, (3,), tile, pieces)

    sweep(odd, [0, 3], lambda d: (u2, (plane_at(d, odd),)), coefs, margins, none, none, sink, (0, rows // ROWS))
    beside[3, rows:] = jnp.zeros(beside[3, rows:].shape, jnp.float32)
    for step, field in enumerate((u0, u1, u2)):
        beside[step] = field[plane_at(3, odd)]


def gain_kernel(kappa, velocity, gain):
    odd = parity("gx")
    p = plane_at(0, odd)

    def body(tile, carry):
        both = zip(load(kappa, (p,), tile), load(velocity, (p,), tile))
        store(gain, (), tile, [far * (k + pick(odd, jnp.zeros_like(v), v)) for k, v in both])
        return carry

    lax.fori_loop(0, kappa.shape[1] // ROWS, body, 0, unroll=UNROLL)


STATE = {(1, 0): 0, (2, 1): 1, (2, 2): 2, (3, 2): 3, (3, 3): 4, (2, 3): 5}
MORE = {(2, 0): 0, (3, 1): 1}


def stages(odd, u0, u1, state, more, others):
    def at(step, d):
        if (step, d) in others:
            return others[step, d]
        if (step, d) in STATE:
            return state, (STATE[step, d],)
        if (step, d) in MORE:
            return more, (MORE[step, d],)
        return (u0, u1)[step], (plane_at(d, odd),)

    def sink(step):
        def put(d, tile, pieces):
            ref, index = at(step, d)
            store(ref, index, tile, pieces)

        return put

    return lambda step: functools.partial(at, step), sink


def far_kernel(u0, u1, margin, kappa, velocity, rate, near0, beside, state, final3, v1):
    odd = parity("gx")
    tiles = kappa.shape[1] // ROWS
    coefs, margins = coefficients(margin, kappa, velocity, rate)
    source, sink = stages(odd, u0, u1, state, None, {(1, 3): (v1, ())})
    own_rows, edge = (0, tiles), ((0, 0), (tiles,))

    def near(tile):
        return load(near0, (), tile)

    def distant(step):
        return lambda tile: load(beside, (step,), tile)

    def finish(d, tile, pieces):
        store(final3, (), tile, pieces)

    sweep(odd, [0, 3], source(0), coefs, margins, near, distant(0), sink(1), own_rows)
    sweep(odd, [3], source(0), coefs, margins, none, distant(0), sink(1), *edge)
    sweep(odd, [1, 2, 3], source(1), coefs, margins, none, distant(1), sink(2), own_rows)
    sweep(odd, [2, 3], source(1), coefs, margins, none, distant(1), sink(2), *edge)
    sweep(odd, [2, 3], source(2), coefs, margins, none, distant(2), sink(3), own_rows)
    sweep(odd, [3], source(2), coefs, margins, none, distant(2), sink(3), *edge)
    sweep(odd, [3], source(3), coefs, margins, none, distant(3), finish, own_rows)


def near_kernel(kappa, velocity, rate, u1, near1, state, final3, out, more, final2, sem):
    odd = parity("gx")
    copy = pltpu.make_async_copy(final3, out.at[plane_at(3, odd)], sem)
    copy.start()
    own_rows = (0, kappa.shape[1] // ROWS)
    coefs, margins = coefficients(None, kappa, velocity, rate)
    source, sink = stages(odd, None, u1, state, more, {})

    def near(tile):
        return load(near1, (), tile)

    def finish(d, tile, pieces):
        store(final2, (), tile, pieces)

    sweep(odd, [0], source(1), coefs, margins, near, none, sink(2), own_rows)
    sweep(odd, [1], source(2), coefs, margins, none, none, sink(3), own_rows)
    sweep(odd, [2], source(3), coefs, margins, none, none, finish, own_rows)
    copy.wait()


def fourth_kernel(n_halo, margin, kappa, velocity, rate, u0, u1, near1, near2, state_in, more_in, final2_in, out_in,
                  state, more, final2, out, base, v3, edges, final1, sems):
    del state_in, more_in, final2_in, out_in
    odd, odd_y = parity("gx"), parity("gy")
    rows, lanes = kappa.shape[1:]
    tiles = rows // ROWS
    coefs, margins = coefficients(margin, kappa, velocity, rate)
    zero, one, two = unpacked(n_halo, [near2[rows + i * ROWS : rows + (i + 1) * ROWS] for i in range(n_halo)])
    row = lax.broadcasted_iota(jnp.int32, (ROWS, lanes), 0)
    top, bottom = row == 0, row == ROWS - 1
    if n_halo == 1:
        top, bottom = jnp.logical_and(top, odd_y == 1), jnp.logical_and(bottom, odd_y == 0)
    outer = pltpu.roll(zero, HALO, 0)
    edges[0] = zero
    edges[1] = one
    edges[2] = two
    edges[3] = jnp.where(top, outer, near1[:ROWS])
    edges[4] = jnp.where(bottom, outer, near1[rows - ROWS :])
    source, sink = stages(odd, u0, u1, state, more, {(3, 0): (v3, ())})
    copies = [pltpu.make_async_copy(final2, out.at[plane_at(2, odd)], sems.at[0]),
              pltpu.make_async_copy(final1, out.at[plane_at(1, odd)], sems.at[1])]

    def near(step):
        def piece(tile):
            if step == 1 and isinstance(tile, int) and tile < tiles:
                return load(edges, (4 if tile else 3,), 0)
            if isinstance(tile, int) and tile == tiles:
                return load(edges, (step,), 0)
            return load(near2, (), tile)

        return piece

    def finish(d, tile, pieces):
        store({0: base, 1: final1, 2: final2}[d], (), tile, pieces)

    own_rows, margin_only, outer_tiles = (0, tiles), ((0, 0), (tiles,)), ((0, 0), (0, tiles - 1, tiles))
    sweep(odd, [0], source(0), coefs, margins, near(0), none, sink(1), *margin_only)
    sweep(odd, [0], source(1), coefs, margins, near(1), none, sink(2), *outer_tiles)
    sweep(odd, [1], source(1), coefs, margins, none, none, sink(2), *margin_only)
    sweep(odd, [1], source(2), coefs, margins, none, none, sink(3), *outer_tiles)
    sweep(odd, [2], source(2), coefs, margins, none, none, sink(3), *margin_only)
    sweep(odd, [2], source(3), coefs, margins, none, none, finish, (0, 0), (0, tiles - 1))
    copies[0].start()
    sweep(odd, [0], source(2), coefs, margins, near(2), none, sink(3), own_rows, (tiles,))
    sweep(odd, [1], source(3), coefs, margins, none, none, finish, own_rows)
    copies[1].start()
    sweep(odd, [0], source(3), coefs, margins, none, none, finish, own_rows)
    for copy in copies:
        copy.wait()


def last_kernel(base, gain, near3, out_in, out, done, sems):
    del out_in
    odd = parity("gx")
    rows = base.shape[0]
    part = rows // PARTS
    copies = []
    for i in range(PARTS):
        span = pl.ds(i * part, part)
        done[span] = base[span] + gain[span] * near3[span]
        copies.append(pltpu.make_async_copy(done.at[span], out.at[plane_at(0, odd), span], sems.at[i]))
        copies[-1].start()
    for copy in copies:
        copy.wait()


def pairs(count, first, wrap):
    out = []
    for i in range(first, count, 2):
        if i + 1 < count or wrap:
            out += [(i, (i + 1) % count), ((i + 1) % count, i)]
    return out


def f32(*shape):
    return jax.ShapeDtypeStruct(shape, jnp.float32)


def call(kernel, out_shape, in_specs, out_specs, scratch=(), aliases=None, weight=0, limit=12):
    return pl.pallas_call(
        kernel,
        out_shape=out_shape,
        in_specs=in_specs,
        out_specs=out_specs,
        scratch_shapes=scratch,
        input_output_aliases=aliases or {},
        cost_estimate=pl.CostEstimate(flops=int(weight * 1e9), bytes_accessed=int(weight * 3.0e6), transcendentals=0),
        compiler_params=pltpu.CompilerParams(vmem_limit_bytes=limit * 1024 * 1024),
    )


def local(initial, kappa, velocity, rate):
    planes, rows, lanes = initial.shape
    full = rows + ROWS
    count_y = lax.axis_size("gy")
    count_x = lax.axis_size("gx")
    n_halo = 1 if count_y == 2 else 2
    chips = pairs(count_x, 1, True)
    cores = pairs(count_x, 0, False)
    rows_pairs = [pairs(count_y, 0, False), pairs(count_y, 1, False)][:n_halo]
    block, wide, plane, wide_plane = f32(planes, rows, lanes), f32(planes, full, lanes), f32(rows, lanes), f32(full, lanes)

    def scratch(*shape):
        return pltpu.VMEM(shape, jnp.float32)

    fields = [pltpu.with_memory_space_constraint(x, pltpu.HBM) for x in (initial, kappa, velocity, rate)]
    message0 = call(plane_kernel, plane, [HBM], ANY, [pltpu.SemaphoreType.DMA((PARTS,))], weight=WEIGHTS[0])(fields[0])
    near0 = lax.ppermute(message0, "gx", chips)
    fields[0], message0 = lax.optimization_barrier((fields[0], message0))
    u0, u1, *rest = call(
        functools.partial(load_kernel, n_halo),
        [wide, wide, block, block, block, plane] + [f32(16, HALO, lanes)] * n_halo,
        [HBM] * 4,
        [VMEM] * (6 + n_halo),
        [scratch(4, 2, planes, ROWS, lanes), pltpu.SemaphoreType.DMA((13,))],
        weight=WEIGHTS[1],
    )(*fields)
    coefs, message1, halos = rest[:3], rest[3], rest[4:]
    halos = [lax.ppermute(halo, "gy", which) for halo, which in zip(halos, rows_pairs)]
    near1 = lax.ppermute(message1, "gx", chips)
    u0, u1, *coefs, u2 = call(
        inner_kernel,
        [wide, wide, block, block, block, wide],
        [HBM] * 4 + [VMEM] * 5,
        [VMEM] * 6,
        [pltpu.SemaphoreType.DMA((4, planes))],
        {4: 0, 5: 1, 6: 2, 7: 3, 8: 4},
        weight=WEIGHTS[2],
    )(*fields, u0, u1, *coefs)
    u0, u1, u2, margin, message2 = call(
        functools.partial(first_kernel, n_halo),
        [wide, wide, wide, f32(3, planes, ROWS, lanes), f32(rows + ROWS * n_halo, lanes)],
        [VMEM] * (6 + n_halo),
        [VMEM] * 5,
        aliases={0: 0, 1: 1, 2: 2},
        weight=WEIGHTS[3],
    )(u0, u1, u2, *coefs, *halos)
    message3, beside = call(
        second_kernel,
        [plane, f32(4, full, lanes)],
        [VMEM] * 7,
        [VMEM] * 2,
        weight=WEIGHTS[4],
    )(u0, u1, u2, margin, *coefs)
    beside, near0 = lax.optimization_barrier((beside, near0))
    beside = lax.ppermute(beside, "gx", cores)
    near2 = lax.ppermute(message2, "gx", chips)
    near3 = lax.ppermute(message3, "gx", chips)
    gain = call(gain_kernel, plane, [VMEM] * 2, VMEM, weight=WEIGHTS[5])(*coefs[:2])
    state, final3 = call(
        far_kernel,
        [f32(len(STATE), full, lanes), plane],
        [VMEM] * 8,
        [VMEM] * 2,
        [scratch(full, lanes)],
        weight=WEIGHTS[6],
    )(u0, u1, margin, *coefs, near0, beside)
    out, more, final2 = call(
        near_kernel,
        [block, f32(2, full, lanes), plane],
        [VMEM] * 7,
        [ANY, VMEM, VMEM],
        [pltpu.SemaphoreType.DMA],
        weight=WEIGHTS[7],
    )(*coefs, u1, near1, state, final3)
    state, more, final2, out, base = call(
        functools.partial(fourth_kernel, n_halo),
        [f32(len(STATE), full, lanes), f32(2, full, lanes), plane, block, plane],
        [VMEM] * 11 + [ANY],
        [VMEM] * 3 + [ANY, VMEM],
        [scratch(full, lanes), scratch(5, ROWS, lanes), scratch(rows, lanes), pltpu.SemaphoreType.DMA((2,))],
        {8: 0, 9: 1, 10: 2, 11: 3},
        weight=WEIGHTS[8],
    )(margin, *coefs, u0, u1, near1, near2, state, more, final2, out)
    return call(
        last_kernel,
        block,
        [VMEM] * 3 + [ANY],
        ANY,
        [scratch(rows, lanes), pltpu.SemaphoreType.DMA((PARTS,))],
        {3: 0},
        weight=WEIGHTS[9],
    )(base, gain, near3, out)


def solution(mesh):
    placed = P("gx", "gy", None)
    return jax.shard_map(local, mesh=mesh, in_specs=(placed,) * 4, out_specs=placed, check_vma=False)
```

```python
import functools

import jax
import jax.numpy as jnp
from jax import lax
from jax.experimental import pallas as pl
from jax.experimental.pallas import tpu as pltpu
from jax.sharding import PartitionSpec as P

robin_p = 0.6
own = (1.0 - robin_p / 2) / (1.0 + robin_p / 2)
far = ((1.0 - own) + robin_p * (1.0 + own) / 2) / (1.0 + robin_p / 2)

VMEM = pl.BlockSpec(memory_space=pltpu.VMEM)
ANY = pl.BlockSpec(memory_space=pl.ANY)
HBM = pl.BlockSpec(memory_space=pltpu.HBM)
HALO = 4
WEIGHTS = (1, 1, 20, 1, 60, 20, 0, 0, 0, 0)
ROWS = 8
LANES = 128
PARTS = 4
UNROLL = 4
GROUPS = (8, 8, 4, 4)


def parity(axis):
    return lax.rem(lax.axis_index(axis), 2)


def plane_at(d, odd):
    return d + odd * (3 - 2 * d)


def pick(odd, yes, no):
    return jnp.where(jnp.broadcast_to(odd == 1, yes.shape), yes, no)


def load(ref, index, tile):
    rows = pl.ds(tile * ROWS if isinstance(tile, int) else pl.multiple_of(tile * ROWS, ROWS), ROWS)
    return [ref[*index, rows, k : k + LANES] for k in range(0, ref.shape[-1], LANES)]


def store(ref, index, tile, pieces):
    rows = pl.ds(tile * ROWS if isinstance(tile, int) else pl.multiple_of(tile * ROWS, ROWS), ROWS)
    for k, piece in enumerate(pieces):
        ref[*index, rows, k * LANES : (k + 1) * LANES] = piece


def ghost(mine, received=None):
    if received is None:
        return [m * own for m in mine]
    return [r * far + m * own for r, m in zip(received, mine)]


def updated(odd, cur, before, after, toward, away, kappa, velocity, rate):
    row = lax.broadcasted_iota(jnp.int32, (ROWS, LANES), 0)
    lane = lax.broadcasted_iota(jnp.int32, (ROWS, LANES), 1)
    zero = jnp.zeros((ROWS, LANES), jnp.float32)
    out = []
    for k, c in enumerate(cur):
        up = pltpu.roll(jnp.where(row == ROWS - 1, before[k], c), 1, 0)
        down = pltpu.roll(jnp.where(row == 0, after[k], c), ROWS - 1, 0)
        low = cur[k - 1] if k else zero
        high = cur[k + 1] if k + 1 < len(cur) else zero
        left = pltpu.roll(jnp.where(lane == LANES - 1, low, c), 1, 1)
        right = pltpu.roll(jnp.where(lane == 0, high, c), LANES - 1, 1)
        minus_x = pick(odd, away[k], toward[k]) if toward is not None else away[k]
        lap = away[k] + toward[k]
        lap = lap + up + down
        lap = lap + left + right
        lap = lap - 6.0 * c
        square = c * c
        bottom = 1.0 + square
        inverse = pl.reciprocal(bottom, approx=True)
        inverse = inverse * (2.0 - bottom * inverse)
        react = rate[k] * c * (square * inverse)
        out.append(c + kappa[k] * lap - velocity[k] * (c - minus_x) - react)
    return out


def sweep(odd, wanted, source, coefs, margins, near, distant, sink, inner, edges=()):
    needed = sorted({e for d in wanted for e in (d - 1, d, d + 1) if 0 <= e <= 3})
    last = source(wanted[0])[0].shape[-2] // ROWS - 1

    def work(tiles, together):
        state = {(d, i): load(*source(d), tile) for i, tile in enumerate(tiles) for d in needed}
        results = []
        for i, tile in enumerate(tiles):
            if isinstance(tile, int):
                before, after = (tile or last + 1) - 1, (tile + 1) % (last + 1)
            else:
                before, after = tile - 1, tile + 1
                if inner[0] == 0 and i == 0:
                    before = lax.select(tile == 0, last, before)
            refs, at = (margins, 0) if isinstance(tile, int) and tile == last else (coefs, tile)
            for d in wanted:
                cur = state[d, i]
                toward = state[d - 1, i] if d > 0 else ghost(cur, near(tile))
                away = state[d + 1, i] if d < 3 else ghost(cur, distant(tile))
                upper = state[d, i - 1] if together and i > 0 else load(*source(d), before)
                lower = state[d, i + 1] if together and i + 1 < len(tiles) else load(*source(d), after)
                p = plane_at(d, odd)
                kvr = [load(ref, (*lead, p), at) for ref, lead in refs]
                results.append((d, tile, updated(odd, cur, upper, lower, toward, away, *kvr)))
        for d, tile, pieces in results:
            sink(d, tile, pieces)

    count = inner[1] - inner[0]
    if count:
        size = max(n for n in range(1, GROUPS[len(wanted) - 1] + 1) if count % n == 0)

        def loop(index, carry):
            work([inner[0] + index * size + i for i in range(size)], True)
            return carry

        lax.fori_loop(0, count // size, loop, 0)
    if edges:
        work(list(edges), False)


def coefficients(margin, kappa, velocity, rate):
    return [(ref, ()) for ref in (kappa, velocity, rate)], [(margin, (i,)) for i in range(3)]


def none(tile):
    return None


def plane_kernel(initial, plane, sems):
    p = plane_at(0, parity("gx"))
    part = plane.shape[0] // PARTS
    spans = [pl.ds(i * part, part) for i in range(PARTS)]
    copies = [pltpu.make_async_copy(initial.at[p, span], plane.at[span], sems.at[i]) for i, span in enumerate(spans)]
    for copy in copies:
        copy.start()
    for copy in copies:
        copy.wait()


def load_kernel(n_halo, initial, kappa, velocity, rate, u0, u1, kappa_v, velocity_v, rate_v, message, *rest):
    halos, (tiles, sems) = rest[:n_halo], rest[n_halo:]
    odd, odd_y = parity("gx"), parity("gy")
    rows = initial.shape[1]
    own_rows = pl.ds(0, rows)
    near, next_to = plane_at(0, odd), plane_at(1, odd)
    fields = (initial, kappa, velocity, rate)
    copies = [pltpu.make_async_copy(initial.at[p], u0.at[p, own_rows], sems.at[i]) for i, p in enumerate((near, next_to))]
    for f, held in enumerate((kappa_v, velocity_v, rate_v)):
        copies.append(pltpu.make_async_copy(fields[f + 1].at[near], held.at[near], sems.at[2 + f]))
    packs = []
    for f, field in enumerate(fields):
        packs.append(pltpu.make_async_copy(field.at[:, :ROWS, :], tiles.at[f, 0], sems.at[5 + 2 * f]))
        packs.append(pltpu.make_async_copy(field.at[:, rows - ROWS :, :], tiles.at[f, 1], sems.at[6 + 2 * f]))
    for copy in copies + packs:
        copy.start()
    u0[:, rows:, :] = jnp.zeros(u0[:, rows:, :].shape, jnp.float32)
    for copy in copies:
        copy.wait()

    def sink(d, tile, pieces):
        store(u1, (plane_at(d, odd),), tile, pieces)
        store(message, (), tile, pieces)

    coefs = [(ref, ()) for ref in (kappa_v, velocity_v, rate_v)]
    sweep(odd, [0], lambda d: (u0, (plane_at(d, odd),)), coefs, None, none, none, sink, (0, rows // ROWS))
    for copy in packs:
        copy.wait()
    for f in range(4):
        first, last = tiles[f, 0, :, :HALO], tiles[f, 1, :, ROWS - HALO :]
        halos[0][4 * f : 4 * f + 4] = pick(odd_y, first, last)
        if n_halo > 1:
            halos[1][4 * f : 4 * f + 4] = pick(odd_y, last, first)


def inner_kernel(initial, kappa, velocity, rate, u0_in, u1_in, kappa_in, velocity_in, rate_in,
                 u0, u1, kappa_v, velocity_v, rate_v, u2, sems):
    odd = parity("gx")
    for d in (0, 1):
        u0[plane_at(d, odd)] = u0_in[plane_at(d, odd)]
    for now, before in ((u1, u1_in), (kappa_v, kappa_in), (velocity_v, velocity_in), (rate_v, rate_in)):
        now[plane_at(0, odd)] = before[plane_at(0, odd)]
    planes, rows = initial.shape[:2]
    own_rows = pl.ds(0, rows)
    for d in range(2, planes):
        u0[plane_at(d, odd), rows:] = jnp.zeros(u0.shape[1:], jnp.float32)[rows:]
    copies = {}
    for d in range(2, planes):
        p = plane_at(d, odd)
        copies[0, d] = pltpu.make_async_copy(initial.at[p], u0.at[p, own_rows], sems.at[0, d])
    for d in range(1, planes):
        p = plane_at(d, odd)
        for f, (field, held) in enumerate([(kappa, kappa_v), (velocity, velocity_v), (rate, rate_v)]):
            copies[f + 1, d] = pltpu.make_async_copy(field.at[p], held.at[p], sems.at[f + 1, d])
    order = [(0, 2), (1, 1), (2, 1), (3, 1), (0, 3)] + [(f, d) for d in range(2, planes) for f in range(1, 4)]
    for key in order:
        copies[key].start()

    def sink(d, tile, pieces):
        store(u1, (plane_at(d, odd),), tile, pieces)

    coefs = [(ref, ()) for ref in (kappa_v, velocity_v, rate_v)]
    for d in range(1, planes):
        if (0, d + 1) in copies:
            copies[0, d + 1].wait()
        for f in range(1, 4):
            copies[f, d].wait()
        sweep(odd, [d], lambda e: (u0, (plane_at(e, odd),)), coefs, None, none, none, sink, (0, rows // ROWS))

    def sink2(d, tile, pieces):
        store(u2, (plane_at(d, odd),), tile, pieces)

    sweep(odd, [0, 1, 2, 3], lambda d: (u1, (plane_at(d, odd),)), coefs, None, none, none, sink2, (1, rows // ROWS - 1))


def first_kernel(n_halo, u0_in, u1_in, u2_in, kappa, velocity, rate, *rest):
    halos, (u0, u1, u2, margin, message) = rest[:n_halo], rest[n_halo:]
    u0[...] = u0_in[...]
    u1[...] = u1_in[...]
    u2[...] = u2_in[...]
    odd, odd_y = parity("gx"), parity("gy")
    rows = kappa.shape[1]
    for f in range(4):
        one = halos[0][4 * f : 4 * f + 4]
        two = halos[1][4 * f : 4 * f + 4] if n_halo > 1 else jnp.zeros_like(one)
        edge = jnp.concatenate([pick(odd_y, two, one), pick(odd_y, one, two)], axis=1)
        if f == 0:
            u0[:, rows:, :] = edge
        else:
            margin[f - 1] = edge

    def sink(d, tile, pieces):
        store(u1, (plane_at(d, odd),), tile, pieces)

    def sink2(d, tile, pieces):
        store(u2, (plane_at(d, odd),), tile, pieces)

    tiles = rows // ROWS
    outer, every = ((0, 0), (0, tiles - 1, tiles)), [0, 1, 2, 3]
    coefs, margins = coefficients(margin, kappa, velocity, rate)
    sweep(odd, every, lambda d: (u0, (plane_at(d, odd),)), coefs, margins, none, none, sink, *outer)
    sweep(odd, every, lambda d: (u1, (plane_at(d, odd),)), coefs, margins, none, none, sink2, *outer)
    p = plane_at(0, odd)
    row = lax.broadcasted_iota(jnp.int32, (ROWS, u0.shape[2]), 0)
    before = u0[p, rows:]
    before = jnp.where(row == HALO - 1, pltpu.roll(u1[p, rows - ROWS : rows], HALO, 0), before)
    before = jnp.where(row == HALO, pltpu.roll(u1[p, :ROWS], HALO, 0), before)
    message[:rows] = u2[p, :rows]
    for i, part in enumerate(packed(odd_y, n_halo, before, u1[p, rows:], u2[p, rows:])):
        message[rows + i * ROWS : rows + (i + 1) * ROWS] = part


def packed(odd_y, n_halo, zero, one, two):
    row = lax.broadcasted_iota(jnp.int32, zero.shape, 0)
    rest = jnp.where(row == 2, pltpu.roll(two, 2, 0), jnp.where(row == 5, pltpu.roll(two, ROWS - 2, 0), one))
    if n_halo > 1:
        return [zero, rest]
    return [jnp.where(row // HALO == odd_y, zero, pltpu.roll(rest, HALO, 0))]


def unpacked(n_halo, tiles):
    zero, rest = tiles if n_halo > 1 else (tiles[0], pltpu.roll(tiles[0], HALO, 0))
    row = lax.broadcasted_iota(jnp.int32, zero.shape, 0)
    two = jnp.where(row < HALO, pltpu.roll(rest, ROWS - 2, 0), pltpu.roll(rest, 2, 0))
    return zero, rest, two


def second_kernel(u0, u1, u2, margin, kappa, velocity, rate, message3, beside):
    odd = parity("gx")
    rows = kappa.shape[1]
    coefs, margins = coefficients(margin, kappa, velocity, rate)

    def sink(d, tile, pieces):
        if d == 0:
            store(message3, (), tile, pieces)
        else:
            store(beside, (3,), tile, pieces)

    sweep(odd, [0, 3], lambda d: (u2, (plane_at(d, odd),)), coefs, margins, none, none, sink, (0, rows // ROWS))
    beside[3, rows:] = jnp.zeros(beside[3, rows:].shape, jnp.float32)
    for step, field in enumerate((u0, u1, u2)):
        beside[step] = field[plane_at(3, odd)]


def gain_kernel(kappa, velocity, gain):
    odd = parity("gx")
    p = plane_at(0, odd)

    def body(tile, carry):
        both = zip(load(kappa, (p,), tile), load(velocity, (p,), tile))
        store(gain, (), tile, [far * (k + pick(odd, jnp.zeros_like(v), v)) for k, v in both])
        return carry

    lax.fori_loop(0, kappa.shape[1] // ROWS, body, 0, unroll=UNROLL)


STATE = {(1, 0): 0, (2, 1): 1, (2, 2): 2, (3, 2): 3, (3, 3): 4, (2, 3): 5}
MORE = {(2, 0): 0, (3, 1): 1}


def stages(odd, u0, u1, state, more, others):
    def at(step, d):
        if (step, d) in others:
            return others[step, d]
        if (step, d) in STATE:
            return state, (STATE[step, d],)
        if (step, d) in MORE:
            return more, (MORE[step, d],)
        return (u0, u1)[step], (plane_at(d, odd),)

    def sink(step):
        def put(d, tile, pieces):
            ref, index = at(step, d)
            store(ref, index, tile, pieces)

        return put

    return lambda step: functools.partial(at, step), sink


def far_kernel(u0, u1, margin, kappa, velocity, rate, near0, beside, state, final3, v1):
    odd = parity("gx")
    tiles = kappa.shape[1] // ROWS
    coefs, margins = coefficients(margin, kappa, velocity, rate)
    source, sink = stages(odd, u0, u1, state, None, {(1, 3): (v1, ())})
    own_rows, edge = (0, tiles), ((0, 0), (tiles,))

    def near(tile):
        return load(near0, (), tile)

    def distant(step):
        return lambda tile: load(beside, (step,), tile)

    def finish(d, tile, pieces):
        store(final3, (), tile, pieces)

    sweep(odd, [0, 3], source(0), coefs, margins, near, distant(0), sink(1), own_rows)
    sweep(odd, [3], source(0), coefs, margins, none, distant(0), sink(1), *edge)
    sweep(odd, [1, 2, 3], source(1), coefs, margins, none, distant(1), sink(2), own_rows)
    sweep(odd, [2, 3], source(1), coefs, margins, none, distant(1), sink(2), *edge)
    sweep(odd, [2, 3], source(2), coefs, margins, none, distant(2), sink(3), own_rows)
    sweep(odd, [3], source(2), coefs, margins, none, distant(2), sink(3), *edge)
    sweep(odd, [3], source(3), coefs, margins, none, distant(3), finish, own_rows)


def near_kernel(kappa, velocity, rate, u1, near1, state, final3, out, more, final2, sem):
    odd = parity("gx")
    copy = pltpu.make_async_copy(final3, out.at[plane_at(3, odd)], sem)
    copy.start()
    own_rows = (0, kappa.shape[1] // ROWS)
    coefs, margins = coefficients(None, kappa, velocity, rate)
    source, sink = stages(odd, None, u1, state, more, {})

    def near(tile):
        return load(near1, (), tile)

    def finish(d, tile, pieces):
        store(final2, (), tile, pieces)

    sweep(odd, [0], source(1), coefs, margins, near, none, sink(2), own_rows)
    sweep(odd, [1], source(2), coefs, margins, none, none, sink(3), own_rows)
    sweep(odd, [2], source(3), coefs, margins, none, none, finish, own_rows)
    copy.wait()


def fourth_kernel(n_halo, margin, kappa, velocity, rate, u0, u1, near1, near2, state_in, more_in, final2_in, out_in,
                  state, more, final2, out, base, v3, edges, final1, sems):
    state[...] = state_in[...]
    more[...] = more_in[...]
    final2[...] = final2_in[...]
    del out_in
    odd, odd_y = parity("gx"), parity("gy")
    rows, lanes = kappa.shape[1:]
    tiles = rows // ROWS
    coefs, margins = coefficients(margin, kappa, velocity, rate)
    zero, one, two = unpacked(n_halo, [near2[rows + i * ROWS : rows + (i + 1) * ROWS] for i in range(n_halo)])
    row = lax.broadcasted_iota(jnp.int32, (ROWS, lanes), 0)
    top, bottom = row == 0, row == ROWS - 1
    if n_halo == 1:
        top, bottom = jnp.logical_and(top, odd_y == 1), jnp.logical_and(bottom, odd_y == 0)
    outer = pltpu.roll(zero, HALO, 0)
    edges[0] = zero
    edges[1] = one
    edges[2] = two
    edges[3] = jnp.where(top, outer, near1[:ROWS])
    edges[4] = jnp.where(bottom, outer, near1[rows - ROWS :])
    source, sink = stages(odd, u0, u1, state, more, {(3, 0): (v3, ())})
    copies = [pltpu.make_async_copy(final2, out.at[plane_at(2, odd)], sems.at[0]),
              pltpu.make_async_copy(final1, out.at[plane_at(1, odd)], sems.at[1])]

    def near(step):
        def piece(tile):
            if step == 1 and isinstance(tile, int) and tile < tiles:
                return load(edges, (4 if tile else 3,), 0)
            if isinstance(tile, int) and tile == tiles:
                return load(edges, (step,), 0)
            return load(near2, (), tile)

        return piece

    def finish(d, tile, pieces):
        store({0: base, 1: final1, 2: final2}[d], (), tile, pieces)

    own_rows, margin_only, outer_tiles = (0, tiles), ((0, 0), (tiles,)), ((0, 0), (0, tiles - 1, tiles))
    sweep(odd, [0], source(0), coefs, margins, near(0), none, sink(1), *margin_only)
    sweep(odd, [0], source(1), coefs, margins, near(1), none, sink(2), *outer_tiles)
    sweep(odd, [1], source(1), coefs, margins, none, none, sink(2), *margin_only)
    sweep(odd, [1], source(2), coefs, margins, none, none, sink(3), *outer_tiles)
    sweep(odd, [2], source(2), coefs, margins, none, none, sink(3), *margin_only)
    sweep(odd, [2], source(3), coefs, margins, none, none, finish, (0, 0), (0, tiles - 1))
    copies[0].start()
    sweep(odd, [0], source(2), coefs, margins, near(2), none, sink(3), own_rows, (tiles,))
    sweep(odd, [1], source(3), coefs, margins, none, none, finish, own_rows)
    copies[1].start()
    sweep(odd, [0], source(3), coefs, margins, none, none, finish, own_rows)
    for copy in copies:
        copy.wait()


def last_kernel(base, gain, near3, out_in, out, done, sems):
    del out_in
    odd = parity("gx")
    rows = base.shape[0]
    part = rows // PARTS
    copies = []
    for i in range(PARTS):
        span = pl.ds(i * part, part)
        done[span] = base[span] + gain[span] * near3[span]
        copies.append(pltpu.make_async_copy(done.at[span], out.at[plane_at(0, odd), span], sems.at[i]))
        copies[-1].start()
    for copy in copies:
        copy.wait()


def pairs(count, first, wrap):
    out = []
    for i in range(first, count, 2):
        if i + 1 < count or wrap:
            out += [(i, (i + 1) % count), ((i + 1) % count, i)]
    return out


def f32(*shape):
    return jax.ShapeDtypeStruct(shape, jnp.float32)


def call(kernel, out_shape, in_specs, out_specs, scratch=(), aliases=None, weight=0, limit=12):
    return pl.pallas_call(
        kernel,
        out_shape=out_shape,
        in_specs=in_specs,
        out_specs=out_specs,
        scratch_shapes=scratch,
        input_output_aliases=aliases or {},
        cost_estimate=pl.CostEstimate(flops=int(weight * 1e9), bytes_accessed=int(weight * 3.0e6), transcendentals=0),
        compiler_params=pltpu.CompilerParams(vmem_limit_bytes=limit * 1024 * 1024),
    )


def local(initial, kappa, velocity, rate):
    planes, rows, lanes = initial.shape
    full = rows + ROWS
    count_y = lax.axis_size("gy")
    count_x = lax.axis_size("gx")
    n_halo = 1 if count_y == 2 else 2
    chips = pairs(count_x, 1, True)
    cores = pairs(count_x, 0, False)
    rows_pairs = [pairs(count_y, 0, False), pairs(count_y, 1, False)][:n_halo]
    block, wide, plane, wide_plane = f32(planes, rows, lanes), f32(planes, full, lanes), f32(rows, lanes), f32(full, lanes)

    def scratch(*shape):
        return pltpu.VMEM(shape, jnp.float32)

    fields = [pltpu.with_memory_space_constraint(x, pltpu.HBM) for x in (initial, kappa, velocity, rate)]
    message0 = call(plane_kernel, plane, [HBM], ANY, [pltpu.SemaphoreType.DMA((PARTS,))], weight=WEIGHTS[0])(fields[0])
    near0 = lax.ppermute(message0, "gx", chips)
    fields[0], message0 = lax.optimization_barrier((fields[0], message0))
    u0, u1, *rest = call(
        functools.partial(load_kernel, n_halo),
        [wide, wide, block, block, block, plane] + [f32(16, HALO, lanes)] * n_halo,
        [HBM] * 4,
        [VMEM] * (6 + n_halo),
        [scratch(4, 2, planes, ROWS, lanes), pltpu.SemaphoreType.DMA((13,))],
        weight=WEIGHTS[1],
    )(*fields)
    coefs, message1, halos = rest[:3], rest[3], rest[4:]
    halos = [lax.ppermute(halo, "gy", which) for halo, which in zip(halos, rows_pairs)]
    near1 = lax.ppermute(message1, "gx", chips)
    u0, u1, *coefs, u2 = call(
        inner_kernel,
        [wide, wide, block, block, block, wide],
        [HBM] * 4 + [VMEM] * 5,
        [VMEM] * 6,
        [pltpu.SemaphoreType.DMA((4, planes))],
        {4: 0, 5: 1, 6: 2, 7: 3, 8: 4},
        weight=WEIGHTS[2],
    )(*fields, u0, u1, *coefs)
    u0, u1, u2, margin, message2 = call(
        functools.partial(first_kernel, n_halo),
        [wide, wide, wide, f32(3, planes, ROWS, lanes), f32(rows + ROWS * n_halo, lanes)],
        [VMEM] * (6 + n_halo),
        [VMEM] * 5,
        aliases={0: 0, 1: 1, 2: 2},
        weight=WEIGHTS[3],
    )(u0, u1, u2, *coefs, *halos)
    message3, beside = call(
        second_kernel,
        [plane, f32(4, full, lanes)],
        [VMEM] * 7,
        [VMEM] * 2,
        weight=WEIGHTS[4],
    )(u0, u1, u2, margin, *coefs)
    beside, near0 = lax.optimization_barrier((beside, near0))
    beside = lax.ppermute(beside, "gx", cores)
    near2 = lax.ppermute(message2, "gx", chips)
    near3 = lax.ppermute(message3, "gx", chips)
    gain = call(gain_kernel, plane, [VMEM] * 2, VMEM, weight=WEIGHTS[5])(*coefs[:2])
    state, final3 = call(
        far_kernel,
        [f32(len(STATE), full, lanes), plane],
        [VMEM] * 8,
        [VMEM] * 2,
        [scratch(full, lanes)],
        weight=WEIGHTS[6],
    )(u0, u1, margin, *coefs, near0, beside)
    out, more, final2 = call(
        near_kernel,
        [block, f32(2, full, lanes), plane],
        [VMEM] * 7,
        [ANY, VMEM, VMEM],
        [pltpu.SemaphoreType.DMA],
        weight=WEIGHTS[7],
    )(*coefs, u1, near1, state, final3)
    state, more, final2, out, base = call(
        functools.partial(fourth_kernel, n_halo),
        [f32(len(STATE), full, lanes), f32(2, full, lanes), plane, block, plane],
        [VMEM] * 11 + [ANY],
        [VMEM] * 3 + [ANY, VMEM],
        [scratch(full, lanes), scratch(5, ROWS, lanes), scratch(rows, lanes), pltpu.SemaphoreType.DMA((2,))],
        {8: 0, 9: 1, 10: 2, 11: 3},
        weight=WEIGHTS[8],
    )(margin, *coefs, u0, u1, near1, near2, state, more, final2, out)
    return call(
        last_kernel,
        block,
        [VMEM] * 3 + [ANY],
        ANY,
        [scratch(rows, lanes), pltpu.SemaphoreType.DMA((PARTS,))],
        {3: 0},
        weight=WEIGHTS[9],
    )(base, gain, near3, out)


def solution(mesh):
    placed = P("gx", "gy", None)
    return jax.shard_map(local, mesh=mesh, in_specs=(placed,) * 4, out_specs=placed, check_vma=False)
```

```python
import functools

import jax
import jax.numpy as jnp
from jax import lax
from jax.experimental import pallas as pl
from jax.experimental.pallas import tpu as pltpu
from jax.sharding import PartitionSpec as P

robin_p = 0.6
own = (1.0 - robin_p / 2) / (1.0 + robin_p / 2)
far = ((1.0 - own) + robin_p * (1.0 + own) / 2) / (1.0 + robin_p / 2)

VMEM = pl.BlockSpec(memory_space=pltpu.VMEM)
ANY = pl.BlockSpec(memory_space=pl.ANY)
HBM = pl.BlockSpec(memory_space=pltpu.HBM)
HALO = 4
WEIGHTS = (1, 1, 20, 1, 60, 20, 0, 0, 0, 0)
ROWS = 8
LANES = 128
PARTS = 4
UNROLL = 4
GROUPS = (8, 8, 4, 4)


def parity(axis):
    return lax.rem(lax.axis_index(axis), 2)


def plane_at(d, odd):
    return d + odd * (3 - 2 * d)


def pick(odd, yes, no):
    return jnp.where(jnp.broadcast_to(odd == 1, yes.shape), yes, no)


def load(ref, index, tile):
    rows = pl.ds(tile * ROWS if isinstance(tile, int) else pl.multiple_of(tile * ROWS, ROWS), ROWS)
    return [ref[*index, rows, k : k + LANES] for k in range(0, ref.shape[-1], LANES)]


def store(ref, index, tile, pieces):
    rows = pl.ds(tile * ROWS if isinstance(tile, int) else pl.multiple_of(tile * ROWS, ROWS), ROWS)
    for k, piece in enumerate(pieces):
        ref[*index, rows, k * LANES : (k + 1) * LANES] = piece


def ghost(mine, received=None):
    if received is None:
        return [m * own for m in mine]
    return [r * far + m * own for r, m in zip(received, mine)]


def updated(odd, cur, before, after, toward, away, kappa, velocity, rate):
    row = lax.broadcasted_iota(jnp.int32, (ROWS, LANES), 0)
    lane = lax.broadcasted_iota(jnp.int32, (ROWS, LANES), 1)
    zero = jnp.zeros((ROWS, LANES), jnp.float32)
    out = []
    for k, c in enumerate(cur):
        up = pltpu.roll(jnp.where(row == ROWS - 1, before[k], c), 1, 0)
        down = pltpu.roll(jnp.where(row == 0, after[k], c), ROWS - 1, 0)
        low = cur[k - 1] if k else zero
        high = cur[k + 1] if k + 1 < len(cur) else zero
        left = pltpu.roll(jnp.where(lane == LANES - 1, low, c), 1, 1)
        right = pltpu.roll(jnp.where(lane == 0, high, c), LANES - 1, 1)
        minus_x = pick(odd, away[k], toward[k]) if toward is not None else away[k]
        lap = away[k] + toward[k]
        lap = lap + up + down
        lap = lap + left + right
        lap = lap - 6.0 * c
        square = c * c
        bottom = 1.0 + square
        inverse = pl.reciprocal(bottom, approx=True)
        inverse = inverse * (2.0 - bottom * inverse)
        react = rate[k] * c * (square * inverse)
        out.append(c + kappa[k] * lap - velocity[k] * (c - minus_x) - react)
    return out


def sweep(odd, wanted, source, coefs, margins, near, distant, sink, inner, edges=(), most=None):
    needed = sorted({e for d in wanted for e in (d - 1, d, d + 1) if 0 <= e <= 3})
    last = source(wanted[0])[0].shape[-2] // ROWS - 1

    def work(tiles, together):
        state = {(d, i): load(*source(d), tile) for i, tile in enumerate(tiles) for d in needed}
        results = []
        for i, tile in enumerate(tiles):
            if isinstance(tile, int):
                before, after = (tile or last + 1) - 1, (tile + 1) % (last + 1)
            else:
                before, after = tile - 1, tile + 1
                if inner[0] == 0 and i == 0:
                    before = lax.select(tile == 0, last, before)
            refs, at = (margins, 0) if isinstance(tile, int) and tile == last else (coefs, tile)
            for d in wanted:
                cur = state[d, i]
                toward = state[d - 1, i] if d > 0 else ghost(cur, near(tile))
                away = state[d + 1, i] if d < 3 else ghost(cur, distant(tile))
                upper = state[d, i - 1] if together and i > 0 else load(*source(d), before)
                lower = state[d, i + 1] if together and i + 1 < len(tiles) else load(*source(d), after)
                p = plane_at(d, odd)
                kvr = [load(ref, (*lead, p), at) for ref, lead in refs]
                results.append((d, tile, updated(odd, cur, upper, lower, toward, away, *kvr)))
        for d, tile, pieces in results:
            sink(d, tile, pieces)

    count = inner[1] - inner[0]
    if count:
        size = max(n for n in range(1, (most or GROUPS[len(wanted) - 1]) + 1) if count % n == 0)

        def loop(index, carry):
            work([inner[0] + index * size + i for i in range(size)], True)
            return carry

        lax.fori_loop(0, count // size, loop, 0)
    if edges:
        work(list(edges), False)


def coefficients(margin, kappa, velocity, rate):
    return [(ref, ()) for ref in (kappa, velocity, rate)], [(margin, (i,)) for i in range(3)]


def none(tile):
    return None


def plane_kernel(initial, plane, sems):
    p = plane_at(0, parity("gx"))
    part = plane.shape[0] // PARTS
    spans = [pl.ds(i * part, part) for i in range(PARTS)]
    copies = [pltpu.make_async_copy(initial.at[p, span], plane.at[span], sems.at[i]) for i, span in enumerate(spans)]
    for copy in copies:
        copy.start()
    for copy in copies:
        copy.wait()


def load_kernel(n_halo, initial, kappa, velocity, rate, u0, u1, kappa_v, velocity_v, rate_v, message, *rest):
    halos, (tiles, sems) = rest[:n_halo], rest[n_halo:]
    odd, odd_y = parity("gx"), parity("gy")
    rows = initial.shape[1]
    own_rows = pl.ds(0, rows)
    near, next_to = plane_at(0, odd), plane_at(1, odd)
    fields = (initial, kappa, velocity, rate)
    copies = [pltpu.make_async_copy(initial.at[p], u0.at[p, own_rows], sems.at[i]) for i, p in enumerate((near, next_to))]
    for f, held in enumerate((kappa_v, velocity_v, rate_v)):
        copies.append(pltpu.make_async_copy(fields[f + 1].at[near], held.at[near], sems.at[2 + f]))
    packs = []
    for f, field in enumerate(fields):
        packs.append(pltpu.make_async_copy(field.at[:, :ROWS, :], tiles.at[f, 0], sems.at[5 + 2 * f]))
        packs.append(pltpu.make_async_copy(field.at[:, rows - ROWS :, :], tiles.at[f, 1], sems.at[6 + 2 * f]))
    for copy in copies + packs:
        copy.start()
    u0[:, rows:, :] = jnp.zeros(u0[:, rows:, :].shape, jnp.float32)
    for copy in copies:
        copy.wait()

    def sink(d, tile, pieces):
        store(u1, (plane_at(d, odd),), tile, pieces)
        store(message, (), tile, pieces)

    coefs = [(ref, ()) for ref in (kappa_v, velocity_v, rate_v)]
    sweep(odd, [0], lambda d: (u0, (plane_at(d, odd),)), coefs, None, none, none, sink, (0, rows // ROWS), most=16)
    for copy in packs:
        copy.wait()
    for f in range(4):
        first, last = tiles[f, 0, :, :HALO], tiles[f, 1, :, ROWS - HALO :]
        halos[0][4 * f : 4 * f + 4] = pick(odd_y, first, last)
        if n_halo > 1:
            halos[1][4 * f : 4 * f + 4] = pick(odd_y, last, first)


def inner_kernel(initial, kappa, velocity, rate, u0_in, u1_in, kappa_in, velocity_in, rate_in,
                 u0, u1, kappa_v, velocity_v, rate_v, u2, sems):
    del u0_in, u1_in, kappa_in, velocity_in, rate_in
    odd = parity("gx")
    planes, rows = initial.shape[:2]
    own_rows = pl.ds(0, rows)
    copies = {}
    for d in range(2, planes):
        p = plane_at(d, odd)
        copies[0, d] = pltpu.make_async_copy(initial.at[p], u0.at[p, own_rows], sems.at[0, d])
    for d in range(1, planes):
        p = plane_at(d, odd)
        for f, (field, held) in enumerate([(kappa, kappa_v), (velocity, velocity_v), (rate, rate_v)]):
            copies[f + 1, d] = pltpu.make_async_copy(field.at[p], held.at[p], sems.at[f + 1, d])
    order = [(0, 2), (1, 1), (2, 1), (3, 1), (0, 3)] + [(f, d) for d in range(2, planes) for f in range(1, 4)]
    for key in order:
        copies[key].start()

    def sink(d, tile, pieces):
        store(u1, (plane_at(d, odd),), tile, pieces)

    coefs = [(ref, ()) for ref in (kappa_v, velocity_v, rate_v)]
    for d in range(1, planes):
        if (0, d + 1) in copies:
            copies[0, d + 1].wait()
        for f in range(1, 4):
            copies[f, d].wait()
        sweep(odd, [d], lambda e: (u0, (plane_at(e, odd),)), coefs, None, none, none, sink, (0, rows // ROWS), most=16)

    def sink2(d, tile, pieces):
        store(u2, (plane_at(d, odd),), tile, pieces)

    sweep(odd, [0, 1, 2, 3], lambda d: (u1, (plane_at(d, odd),)), coefs, None, none, none, sink2, (1, rows // ROWS - 1))


def first_kernel(n_halo, u0_in, u1_in, u2_in, kappa, velocity, rate, *rest):
    del u0_in, u1_in, u2_in
    halos, (u0, u1, u2, margin, message) = rest[:n_halo], rest[n_halo:]
    odd, odd_y = parity("gx"), parity("gy")
    rows = kappa.shape[1]
    for f in range(4):
        one = halos[0][4 * f : 4 * f + 4]
        two = halos[1][4 * f : 4 * f + 4] if n_halo > 1 else jnp.zeros_like(one)
        edge = jnp.concatenate([pick(odd_y, two, one), pick(odd_y, one, two)], axis=1)
        if f == 0:
            u0[:, rows:, :] = edge
        else:
            margin[f - 1] = edge

    def sink(d, tile, pieces):
        store(u1, (plane_at(d, odd),), tile, pieces)

    def sink2(d, tile, pieces):
        store(u2, (plane_at(d, odd),), tile, pieces)

    tiles = rows // ROWS
    outer, every = ((0, 0), (0, tiles - 1, tiles)), [0, 1, 2, 3]
    coefs, margins = coefficients(margin, kappa, velocity, rate)
    sweep(odd, every, lambda d: (u0, (plane_at(d, odd),)), coefs, margins, none, none, sink, *outer)
    sweep(odd, every, lambda d: (u1, (plane_at(d, odd),)), coefs, margins, none, none, sink2, *outer)
    p = plane_at(0, odd)
    row = lax.broadcasted_iota(jnp.int32, (ROWS, u0.shape[2]), 0)
    before = u0[p, rows:]
    before = jnp.where(row == HALO - 1, pltpu.roll(u1[p, rows - ROWS : rows], HALO, 0), before)
    before = jnp.where(row == HALO, pltpu.roll(u1[p, :ROWS], HALO, 0), before)
    message[:rows] = u2[p, :rows]
    for i, part in enumerate(packed(odd_y, n_halo, before, u1[p, rows:], u2[p, rows:])):
        message[rows + i * ROWS : rows + (i + 1) * ROWS] = part


def packed(odd_y, n_halo, zero, one, two):
    row = lax.broadcasted_iota(jnp.int32, zero.shape, 0)
    rest = jnp.where(row == 2, pltpu.roll(two, 2, 0), jnp.where(row == 5, pltpu.roll(two, ROWS - 2, 0), one))
    if n_halo > 1:
        return [zero, rest]
    return [jnp.where(row // HALO == odd_y, zero, pltpu.roll(rest, HALO, 0))]


def unpacked(n_halo, tiles):
    zero, rest = tiles if n_halo > 1 else (tiles[0], pltpu.roll(tiles[0], HALO, 0))
    row = lax.broadcasted_iota(jnp.int32, zero.shape, 0)
    two = jnp.where(row < HALO, pltpu.roll(rest, ROWS - 2, 0), pltpu.roll(rest, 2, 0))
    return zero, rest, two


def second_kernel(u0, u1, u2, margin, kappa, velocity, rate, message3, beside):
    odd = parity("gx")
    rows = kappa.shape[1]
    coefs, margins = coefficients(margin, kappa, velocity, rate)

    def sink(d, tile, pieces):
        if d == 0:
            store(message3, (), tile, pieces)
        else:
            store(beside, (3,), tile, pieces)

    sweep(odd, [0, 3], lambda d: (u2, (plane_at(d, odd),)), coefs, margins, none, none, sink, (0, rows // ROWS), most=16)
    beside[3, rows:] = jnp.zeros(beside[3, rows:].shape, jnp.float32)
    for step, field in enumerate((u0, u1, u2)):
        beside[step] = field[plane_at(3, odd)]


def gain_kernel(kappa, velocity, gain):
    odd = parity("gx")
    p = plane_at(0, odd)

    def body(tile, carry):
        both = zip(load(kappa, (p,), tile), load(velocity, (p,), tile))
        store(gain, (), tile, [far * (k + pick(odd, jnp.zeros_like(v), v)) for k, v in both])
        return carry

    lax.fori_loop(0, kappa.shape[1] // ROWS, body, 0, unroll=UNROLL)


STATE = {(1, 0): 0, (2, 1): 1, (2, 2): 2, (3, 2): 3, (3, 3): 4, (2, 3): 5}
MORE = {(2, 0): 0, (3, 1): 1}


def stages(odd, u0, u1, state, more, others):
    def at(step, d):
        if (step, d) in others:
            return others[step, d]
        if (step, d) in STATE:
            return state, (STATE[step, d],)
        if (step, d) in MORE:
            return more, (MORE[step, d],)
        return (u0, u1)[step], (plane_at(d, odd),)

    def sink(step):
        def put(d, tile, pieces):
            ref, index = at(step, d)
            store(ref, index, tile, pieces)

        return put

    return lambda step: functools.partial(at, step), sink


def far_kernel(u0, u1, margin, kappa, velocity, rate, near0, beside, state, final3, v1):
    odd = parity("gx")
    tiles = kappa.shape[1] // ROWS
    coefs, margins = coefficients(margin, kappa, velocity, rate)
    source, sink = stages(odd, u0, u1, state, None, {(1, 3): (v1, ())})
    own_rows, edge = (0, tiles), ((0, 0), (tiles,))

    def near(tile):
        return load(near0, (), tile)

    def distant(step):
        return lambda tile: load(beside, (step,), tile)

    def finish(d, tile, pieces):
        store(final3, (), tile, pieces)

    sweep(odd, [0, 3], source(0), coefs, margins, near, distant(0), sink(1), own_rows)
    sweep(odd, [3], source(0), coefs, margins, none, distant(0), sink(1), *edge)
    sweep(odd, [1, 2, 3], source(1), coefs, margins, none, distant(1), sink(2), own_rows)
    sweep(odd, [2, 3], source(1), coefs, margins, none, distant(1), sink(2), *edge)
    sweep(odd, [2, 3], source(2), coefs, margins, none, distant(2), sink(3), own_rows)
    sweep(odd, [3], source(2), coefs, margins, none, distant(2), sink(3), *edge)
    sweep(odd, [3], source(3), coefs, margins, none, distant(3), finish, own_rows, most=16)


def near_kernel(kappa, velocity, rate, u1, near1, state, final3, out, more, final2, sem):
    odd = parity("gx")
    copy = pltpu.make_async_copy(final3, out.at[plane_at(3, odd)], sem)
    copy.start()
    own_rows = (0, kappa.shape[1] // ROWS)
    coefs, margins = coefficients(None, kappa, velocity, rate)
    source, sink = stages(odd, None, u1, state, more, {})

    def near(tile):
        return load(near1, (), tile)

    def finish(d, tile, pieces):
        store(final2, (), tile, pieces)

    sweep(odd, [0], source(1), coefs, margins, near, none, sink(2), own_rows)
    sweep(odd, [1], source(2), coefs, margins, none, none, sink(3), own_rows)
    sweep(odd, [2], source(3), coefs, margins, none, none, finish, own_rows)
    copy.wait()


def fourth_kernel(n_halo, margin, kappa, velocity, rate, u0, u1, near1, near2, state_in, more_in, final2_in, out_in,
                  state, more, final2, out, base, v3, edges, final1, sems):
    del state_in, more_in, final2_in, out_in
    odd, odd_y = parity("gx"), parity("gy")
    rows, lanes = kappa.shape[1:]
    tiles = rows // ROWS
    coefs, margins = coefficients(margin, kappa, velocity, rate)
    zero, one, two = unpacked(n_halo, [near2[rows + i * ROWS : rows + (i + 1) * ROWS] for i in range(n_halo)])
    row = lax.broadcasted_iota(jnp.int32, (ROWS, lanes), 0)
    top, bottom = row == 0, row == ROWS - 1
    if n_halo == 1:
        top, bottom = jnp.logical_and(top, odd_y == 1), jnp.logical_and(bottom, odd_y == 0)
    outer = pltpu.roll(zero, HALO, 0)
    edges[0] = zero
    edges[1] = one
    edges[2] = two
    edges[3] = jnp.where(top, outer, near1[:ROWS])
    edges[4] = jnp.where(bottom, outer, near1[rows - ROWS :])
    source, sink = stages(odd, u0, u1, state, more, {(3, 0): (v3, ())})
    copies = [pltpu.make_async_copy(final2, out.at[plane_at(2, odd)], sems.at[0]),
              pltpu.make_async_copy(final1, out.at[plane_at(1, odd)], sems.at[1])]

    def near(step):
        def piece(tile):
            if step == 1 and isinstance(tile, int) and tile < tiles:
                return load(edges, (4 if tile else 3,), 0)
            if isinstance(tile, int) and tile == tiles:
                return load(edges, (step,), 0)
            return load(near2, (), tile)

        return piece

    def finish(d, tile, pieces):
        store({0: base, 1: final1, 2: final2}[d], (), tile, pieces)

    own_rows, margin_only, outer_tiles = (0, tiles), ((0, 0), (tiles,)), ((0, 0), (0, tiles - 1, tiles))
    sweep(odd, [0], source(0), coefs, margins, near(0), none, sink(1), *margin_only)
    sweep(odd, [0], source(1), coefs, margins, near(1), none, sink(2), *outer_tiles)
    sweep(odd, [1], source(1), coefs, margins, none, none, sink(2), *margin_only)
    sweep(odd, [1], source(2), coefs, margins, none, none, sink(3), *outer_tiles)
    sweep(odd, [2], source(2), coefs, margins, none, none, sink(3), *margin_only)
    sweep(odd, [2], source(3), coefs, margins, none, none, finish, (0, 0), (0, tiles - 1))
    copies[0].start()
    sweep(odd, [0], source(2), coefs, margins, near(2), none, sink(3), own_rows, (tiles,))
    sweep(odd, [1], source(3), coefs, margins, none, none, finish, own_rows)
    copies[1].start()
    sweep(odd, [0], source(3), coefs, margins, none, none, finish, own_rows)
    for copy in copies:
        copy.wait()


def last_kernel(base, gain, near3, out_in, out, done, sems):
    del out_in
    odd = parity("gx")
    rows = base.shape[0]
    part = rows // PARTS
    copies = []
    for i in range(PARTS):
        span = pl.ds(i * part, part)
        done[span] = base[span] + gain[span] * near3[span]
        copies.append(pltpu.make_async_copy(done.at[span], out.at[plane_at(0, odd), span], sems.at[i]))
        copies[-1].start()
    for copy in copies:
        copy.wait()


def pairs(count, first, wrap):
    out = []
    for i in range(first, count, 2):
        if i + 1 < count or wrap:
            out += [(i, (i + 1) % count), ((i + 1) % count, i)]
    return out


def f32(*shape):
    return jax.ShapeDtypeStruct(shape, jnp.float32)


def call(kernel, out_shape, in_specs, out_specs, scratch=(), aliases=None, weight=0, limit=12):
    return pl.pallas_call(
        kernel,
        out_shape=out_shape,
        in_specs=in_specs,
        out_specs=out_specs,
        scratch_shapes=scratch,
        input_output_aliases=aliases or {},
        cost_estimate=pl.CostEstimate(flops=int(weight * 1e9), bytes_accessed=int(weight * 3.0e6), transcendentals=0),
        compiler_params=pltpu.CompilerParams(vmem_limit_bytes=limit * 1024 * 1024),
    )


def local(initial, kappa, velocity, rate):
    planes, rows, lanes = initial.shape
    full = rows + ROWS
    count_y = lax.axis_size("gy")
    count_x = lax.axis_size("gx")
    n_halo = 1 if count_y == 2 else 2
    chips = pairs(count_x, 1, True)
    cores = pairs(count_x, 0, False)
    rows_pairs = [pairs(count_y, 0, False), pairs(count_y, 1, False)][:n_halo]
    block, wide, plane, wide_plane = f32(planes, rows, lanes), f32(planes, full, lanes), f32(rows, lanes), f32(full, lanes)

    def scratch(*shape):
        return pltpu.VMEM(shape, jnp.float32)

    fields = [pltpu.with_memory_space_constraint(x, pltpu.HBM) for x in (initial, kappa, velocity, rate)]
    message0 = call(plane_kernel, plane, [HBM], ANY, [pltpu.SemaphoreType.DMA((PARTS,))], weight=WEIGHTS[0])(fields[0])
    near0 = lax.ppermute(message0, "gx", chips)
    fields[0], message0 = lax.optimization_barrier((fields[0], message0))
    u0, u1, *rest = call(
        functools.partial(load_kernel, n_halo),
        [wide, wide, block, block, block, plane] + [f32(16, HALO, lanes)] * n_halo,
        [HBM] * 4,
        [VMEM] * (6 + n_halo),
        [scratch(4, 2, planes, ROWS, lanes), pltpu.SemaphoreType.DMA((13,))],
        weight=WEIGHTS[1],
    )(*fields)
    coefs, message1, halos = rest[:3], rest[3], rest[4:]
    halos = [lax.ppermute(halo, "gy", which) for halo, which in zip(halos, rows_pairs)]
    near1 = lax.ppermute(message1, "gx", chips)
    u0, u1, *coefs, u2 = call(
        inner_kernel,
        [wide, wide, block, block, block, wide],
        [HBM] * 4 + [VMEM] * 5,
        [VMEM] * 6,
        [pltpu.SemaphoreType.DMA((4, planes))],
        {4: 0, 5: 1, 6: 2, 7: 3, 8: 4},
        weight=WEIGHTS[2],
    )(*fields, u0, u1, *coefs)
    u0, u1, u2, margin, message2 = call(
        functools.partial(first_kernel, n_halo),
        [wide, wide, wide, f32(3, planes, ROWS, lanes), f32(rows + ROWS * n_halo, lanes)],
        [VMEM] * (6 + n_halo),
        [VMEM] * 5,
        aliases={0: 0, 1: 1, 2: 2},
        weight=WEIGHTS[3],
    )(u0, u1, u2, *coefs, *halos)
    message3, beside = call(
        second_kernel,
        [plane, f32(4, full, lanes)],
        [VMEM] * 7,
        [VMEM] * 2,
        weight=WEIGHTS[4],
    )(u0, u1, u2, margin, *coefs)
    beside, near0 = lax.optimization_barrier((beside, near0))
    beside = lax.ppermute(beside, "gx", cores)
    near2 = lax.ppermute(message2, "gx", chips)
    near3 = lax.ppermute(message3, "gx", chips)
    gain = call(gain_kernel, plane, [VMEM] * 2, VMEM, weight=WEIGHTS[5])(*coefs[:2])
    state, final3 = call(
        far_kernel,
        [f32(len(STATE), full, lanes), plane],
        [VMEM] * 8,
        [VMEM] * 2,
        [scratch(full, lanes)],
        weight=WEIGHTS[6],
    )(u0, u1, margin, *coefs, near0, beside)
    out, more, final2 = call(
        near_kernel,
        [block, f32(2, full, lanes), plane],
        [VMEM] * 7,
        [ANY, VMEM, VMEM],
        [pltpu.SemaphoreType.DMA],
        weight=WEIGHTS[7],
    )(*coefs, u1, near1, state, final3)
    state, more, final2, out, base = call(
        functools.partial(fourth_kernel, n_halo),
        [f32(len(STATE), full, lanes), f32(2, full, lanes), plane, block, plane],
        [VMEM] * 11 + [ANY],
        [VMEM] * 3 + [ANY, VMEM],
        [scratch(full, lanes), scratch(5, ROWS, lanes), scratch(rows, lanes), pltpu.SemaphoreType.DMA((2,))],
        {8: 0, 9: 1, 10: 2, 11: 3},
        weight=WEIGHTS[8],
    )(margin, *coefs, u0, u1, near1, near2, state, more, final2, out)
    return call(
        last_kernel,
        block,
        [VMEM] * 3 + [ANY],
        ANY,
        [scratch(rows, lanes), pltpu.SemaphoreType.DMA((PARTS,))],
        {3: 0},
        weight=WEIGHTS[9],
    )(base, gain, near3, out)


def solution(mesh):
    placed = P("gx", "gy", None)
    return jax.shard_map(local, mesh=mesh, in_specs=(placed,) * 4, out_specs=placed, check_vma=False)
```
